512 devices in a mesh: ctx: 64 (over x, z, core), ch: 8 (over y).
Axes of the slice: x: 4, y: 8, z: 8, core: 2. Of those that a mesh axis runs over, the one named last changes fastest.
Arguments:
- q_in: bfloat16 [8192, 4096], P('ctx', 'ch'), may hold values from -6 to 6
- k_in: bfloat16 [8192, 4096], P('ctx', 'ch'), may hold values from -6 to 6
- v_in: bfloat16 [8192, 4096], P('ctx', 'ch'), may hold values from -6 to 6
- grad_out: bfloat16 [8192, 4096], P('ctx', 'ch'), may hold values from -30 to 30
- short_filter: float32 [3, 4096], P(None, 'ch'), may hold values from -3 to 3
- kernel: float32 [8192, 4096], P('ctx', 'ch'), may hold values from -0.0625 to 0.0625
- skip: float32 [4096], P('ch'), may hold values from -3 to 3
Outputs:
- mixed: bfloat16 [8192, 4096], P('ctx', 'ch')
- grad_q: bfloat16 [8192, 4096], P('ctx', 'ch')
- grad_k: bfloat16 [8192, 4096], P('ctx', 'ch')
- grad_v: bfloat16 [8192, 4096], P('ctx', 'ch')
- grad_short: float32 [3, 4096], P(None, 'ch')
- grad_skip: float32 [4096], P('ch')
- grad_kernel: float32 [8192, 4096], P('ctx', 'ch')
The draws below stay inside these ranges and needn't reach their ends.
All inputs are finite; a program needn't handle non-finite values.
Results may differ from the reference program's by a relative error of at most 0.009.
Values may be sent and summed in bfloat16 or wider, within the bound.
A program may use at most 64 MiB of HBM per device.

```python
import math
import jax
import jax.numpy as jnp
from jax import lax

D = 4096
SHORT = 3
SEQ = 8192


def draw_grad_out(key, part):
    key_base = jax.random.fold_in(key, 11)
    key_chan = jax.random.fold_in(key, 12)
    key_rows = jax.random.fold_in(key, 13)
    chan_pos = jnp.arange(D).astype(jnp.float32) / D
    chan_noise = jax.random.uniform(key_chan, (D,), jnp.float32)
    row_noise = jax.random.uniform(key_rows, (SEQ,), jnp.float32)
    base = jax.random.truncated_normal(key_base, -3.0, 3.0, (SEQ, D), jnp.float32)
    chan_trend = 0.5 * chan_pos
    log_scale = chan_trend[None, :] + 0.5 * chan_noise[None, :] + 0.5 * row_noise[:, None] - 0.75
    return (base * jnp.exp(log_scale * math.log(10.0))).astype(jnp.bfloat16)


def block_scale(own_key, dims, split, least, high):
    def one(dim, shards_of):
        heights = jax.random.uniform(jax.random.fold_in(jax.random.fold_in(own_key, 6), dim), (shards_of,), jnp.float32, least / len(split), high / len(split))
        return jnp.repeat(jnp.exp(heights), dims[dim] // shards_of).reshape((-1,) + (1,) * (len(dims) - dim - 1))

    gain = one(*split[0])
    for cut in split[1:]:
        gain = gain * one(*cut)
    return gain


def scatter_about(own_key, extent, scale, most, split=(), held_as=jnp.bfloat16):
    drawn = scale * jax.random.normal(own_key, extent, jnp.float32)
    if split:
        drawn = drawn * block_scale(own_key, extent, split, -0.22, 0.18)
    return jnp.clip(drawn, -most, most).astype(held_as)


def setup_inputs(seed: int = 0) -> dict:
    seeds = jax.random.split(jax.random.key(seed), 8)
    q_in = scatter_about(seeds[0], (SEQ, D), 1.0, 6.0, ((0, 64), (1, 8)))
    k_in = scatter_about(seeds[1], (SEQ, D), 1.0, 6.0, ((0, 64), (1, 8)))
    v_in = scatter_about(seeds[2], (SEQ, D), 1.0, 6.0, ((0, 64), (1, 8)))
    grad_out = draw_grad_out(jax.random.fold_in(seeds[7], 71), 0)
    short_filter = scatter_about(seeds[4], (SHORT, D), 0.6, 3.0, ((1, 8),), jnp.float32)
    kernel = scatter_about(seeds[5], (SEQ, D), SEQ ** -0.5, 0.0625, ((0, 64), (1, 8)), jnp.float32)
    skip = scatter_about(seeds[6], (D,), 0.5, 3.0, ((0, 8),), jnp.float32)
    return dict(q_in=q_in, k_in=k_in, v_in=v_in, grad_out=grad_out, short_filter=short_filter, kernel=kernel, skip=skip)


def causal_short(signal, short_taps):
    halo_rows = short_taps.shape[0] - 1
    seq_len = signal.shape[0]
    padded = jnp.concatenate([jnp.zeros((halo_rows, signal.shape[1]), jnp.float32), signal], axis=0)
    result = short_taps[0] * padded[halo_rows:halo_rows + seq_len]
    for shift_idx in range(1, short_taps.shape[0]):
        result = result + short_taps[shift_idx] * padded[halo_rows - shift_idx:halo_rows - shift_idx + seq_len]
    return (result, padded)

def causal_adjoint(signal, short_taps):
    halo_rows = short_taps.shape[0] - 1
    seq_len = signal.shape[0]
    padded = jnp.concatenate([signal, jnp.zeros((halo_rows, signal.shape[1]), jnp.float32)], axis=0)
    result = short_taps[0] * padded[0:seq_len]
    for shift_idx in range(1, short_taps.shape[0]):
        result = result + short_taps[shift_idx] * padded[shift_idx:shift_idx + seq_len]
    return result

def channel_block(q_in, k_in, v_in, grad_out, short_taps, kernel, skip):
    seq_len = q_in.shape[0]
    halo_rows = short_taps.shape[0] - 1
    q_short, q_pad = causal_short(q_in.astype(jnp.float32), short_taps)
    k_short, k_pad = causal_short(k_in.astype(jnp.float32), short_taps)
    v_short, v_pad = causal_short(v_in.astype(jnp.float32), short_taps)
    product = lax.optimization_barrier((k_short * v_short).astype(jnp.bfloat16))
    product_wide = product.astype(jnp.float32)
    fft_len = 2 * seq_len
    spec_prod = jnp.fft.rfft(product_wide, n=fft_len, axis=0)
    spec_kernel = jnp.fft.rfft(kernel, n=fft_len, axis=0)
    conv = jnp.fft.irfft(spec_prod * spec_kernel, n=fft_len, axis=0)[:seq_len]
    filtered = conv + skip[None, :] * product_wide
    mixed = (q_short * filtered).astype(jnp.bfloat16)
    upstream = grad_out.astype(jnp.float32)
    back_q = upstream * filtered
    back_mix = upstream * q_short
    back_cast = lax.optimization_barrier(back_mix.astype(jnp.bfloat16)).astype(jnp.float32)
    spec_back = jnp.fft.rfft(back_cast, n=fft_len, axis=0)
    back_prod = jnp.fft.irfft(jnp.conj(spec_kernel) * spec_back, n=fft_len, axis=0)[:seq_len] + skip[None, :] * back_mix
    kernel_grad = jnp.fft.irfft(jnp.conj(spec_prod) * spec_back, n=fft_len, axis=0)[:seq_len]
    back_k = back_prod * v_short
    back_v = back_prod * k_short
    grad_q = causal_adjoint(back_q, short_taps).astype(jnp.bfloat16)
    grad_k = causal_adjoint(back_k, short_taps).astype(jnp.bfloat16)
    grad_v = causal_adjoint(back_v, short_taps).astype(jnp.bfloat16)
    tap_rows = []
    for shift_idx in range(short_taps.shape[0]):
        first = halo_rows - shift_idx
        tap_rows.append(lax.optimization_barrier(jnp.sum(back_q * q_pad[first:first + seq_len] + back_k * k_pad[first:first + seq_len] + back_v * v_pad[first:first + seq_len], axis=0)))
    short_grad = jnp.stack(tap_rows)
    skip_grad = lax.optimization_barrier(jnp.sum(back_mix * product_wide, axis=0))
    return (mixed, grad_q, grad_k, grad_v, short_grad, skip_grad, kernel_grad)

def run_block(pieces):
    return channel_block(*pieces)

def reference(q_in, k_in, v_in, grad_out, short_filter, kernel, skip):
    seq_len, width_all = q_in.shape
    lanes = 128
    block_count = width_all // lanes

    def split_rows(array):
        return array.reshape(seq_len, block_count, lanes).transpose(1, 0, 2)

    def join_rows(array):
        return array.transpose(1, 0, 2).reshape(seq_len, width_all)
    taps_blocks = short_filter.reshape(short_filter.shape[0], block_count, lanes).transpose(1, 0, 2)
    results = lax.map(run_block, (split_rows(q_in), split_rows(k_in), split_rows(v_in), split_rows(grad_out), taps_blocks, split_rows(kernel), skip.reshape(block_count, lanes)))
    short_grad = results[4].transpose(1, 0, 2).reshape(short_filter.shape[0], width_all)
    skip_grad = results[5].reshape(width_all)
    kernel_grad = join_rows(results[6])
    norm_sq = jnp.sum(short_grad * short_grad) + jnp.sum(skip_grad * skip_grad) + jnp.sum(kernel_grad * kernel_grad)
    clip_limit = math.sqrt(float(seq_len * width_all))
    factor = clip_limit / jnp.maximum(jnp.sqrt(norm_sq), clip_limit)
    return (join_rows(results[0]), join_rows(results[1]), join_rows(results[2]), join_rows(results[3]), factor * short_grad, factor * skip_grad, factor * kernel_grad)
```

```python
import functools
import math

import jax
import jax.numpy as jnp
import numpy as np
from jax import lax
from jax.experimental import pallas as pl
from jax.experimental.pallas import tpu as pltpu
from jax.sharding import PartitionSpec as P

MESH = pl.DeviceIdType.MESH
F32 = jnp.float32
BF16 = jnp.bfloat16
LANES = 128
OWN = 8
HALO, KERN, PROD, BACK, CONV, CORR, LAG, TAIL, SUM1, SUM2, NORM = range(11)


def split_table(table):
    high = table.astype(np.float32).astype(jnp.bfloat16)
    low = (table - high.astype(np.float64)).astype(np.float32).astype(jnp.bfloat16)
    return high, low


def tables(blocks, rows):
    length = blocks * rows
    outer = 2.0 * np.pi * np.outer(np.arange(blocks) + 0.25, np.arange(blocks)) / blocks
    twist = 2.0 * np.pi * np.outer(np.arange(blocks) + 0.25, np.arange(rows)) / length
    inner = 2.0 * np.pi * (np.outer(np.arange(rows), np.arange(rows)) % rows) / rows
    out_f = np.concatenate([np.cos(outer), -np.sin(outer)], axis=0)
    out_i = np.concatenate([np.cos(outer.T), -np.sin(outer.T)], axis=1) / length
    cos, sin = np.cos(inner), np.sin(inner)
    in_f = np.block([[cos, -sin], [sin, cos]])
    in_i = np.block([[cos, sin], [-sin, cos]])
    return (
        np.concatenate(split_table(out_f), axis=1),
        np.concatenate(split_table(out_i), axis=1),
        split_table(in_f)[0],
        split_table(in_i)[0],
        np.cos(twist).astype(np.float32),
        np.sin(twist).astype(np.float32),
    )


def mixer_kernel(
    dims,
    limit,
    q_ref,
    k_ref,
    v_ref,
    go_ref,
    kern_ref,
    taps_ref,
    skip_ref,
    outf_ref,
    outi_ref,
    inf_ref,
    ini_ref,
    tcos_ref,
    tsin_ref,
    mixed_ref,
    gq_ref,
    gk_ref,
    gv_ref,
    gkern_ref,
    small_ref,
    src,
    dst,
    ext,
    wide,
    back,
    hsrc,
    hdst,
    tsrc,
    tdst,
    tmp,
    bbuf,
    spec,
    red,
    red1,
    red2,
    nrm,
    nrmd,
    ssem,
    rsem,
):
    pieces, group_a, group_b, chs = dims
    rows, channels = q_ref.shape
    me = lax.axis_index("ctx")
    ch = lax.axis_index("ch")
    my_a = me // (2 * group_b) * 2 + me % 2
    my_b = me // 2 % group_b

    def ctx_of(a, b):
        return (a // 2 * group_b + b) * 2 + a % 2

    barrier = pltpu.get_barrier_semaphore()

    @pl.loop(1, pieces)
    def _(step):
        peer = lax.rem(me + step, pieces)
        pl.semaphore_signal(barrier, inc=1, device_id=(peer, ch), device_id_type=MESH)

    @pl.loop(1, chs)
    def _(step):
        peer = lax.rem(ch + step, chs)
        pl.semaphore_signal(barrier, inc=1, device_id=(me, peer), device_id_type=MESH)

    def spread(slot):
        @pl.loop(1, pieces)
        def _(step):
            peer = lax.rem(me + step, pieces)
            pltpu.make_async_remote_copy(
                src.at[slot, peer],
                dst.at[slot, me],
                ssem.at[KERN + slot],
                rsem.at[KERN + slot],
                device_id=(peer, ch),
                device_id_type=MESH,
            ).start()

        dst[slot, me] = src[slot, me]

    def arrived(slot):
        view = dst.at[slot, pl.ds(0, pieces - 1)]
        pltpu.make_async_copy(view, view, rsem.at[KERN + slot]).wait()

    def to_pieces(slot, cb, block):
        per = LANES // OWN
        src[slot, cb * per : (cb + 1) * per] = block.T.reshape(per, OWN, rows).astype(BF16)

    def from_pieces(slot, cb):
        per = LANES // OWN
        block = dst[slot, cb * per : (cb + 1) * per].astype(F32)
        return block.reshape(LANES, rows).T

    blocks = [slice(cb * LANES, (cb + 1) * LANES) for cb in range(channels // LANES)]

    for i, ref in enumerate((q_ref, k_ref, v_ref)):
        ext[i, 8 : 8 + rows, :] = ref[...].astype(F32)
        hsrc[2 * i : 2 * i + 2, :] = ext[i, 6 + rows : 8 + rows, :]
    hsrc[6:8, :] = jnp.zeros((2, channels), F32)
    for cb, cs in enumerate(blocks):
        to_pieces(0, cb, kern_ref[:, cs])

    pl.semaphore_wait(barrier, pieces - 1 + chs - 1)

    halo = pltpu.make_async_remote_copy(
        hsrc,
        hdst,
        ssem.at[HALO],
        rsem.at[HALO],
        device_id=(lax.rem(me + 1, pieces), ch),
        device_id_type=MESH,
    )
    halo.start()
    spread(0)
    halo.wait_recv()

    def taps_at(j, cs):
        return taps_ref[j : j + 1, cs]

    def short(i, cs):
        total = taps_at(0, cs) * ext[i, 8 : 8 + rows, cs]
        for j in range(1, 3):
            total = total + taps_at(j, cs) * ext[i, 8 - j : 8 - j + rows, cs]
        return total

    for i in range(3):
        halo_rows = hdst[2 * i : 2 * i + 2, :]
        ext[i, 6:8, :] = jnp.where(me > 0, halo_rows, jnp.zeros_like(halo_rows))
    for cb, cs in enumerate(blocks):
        k_short = short(1, cs)
        v_short = short(2, cs)
        product = (k_short * v_short).astype(BF16).astype(F32)
        wide[1, :, cs] = k_short
        wide[2, :, cs] = v_short
        wide[3, :, cs] = product
        to_pieces(1, cb, product)
    spread(1)
    for cb, cs in enumerate(blocks):
        q_short = short(0, cs)
        back_mix = go_ref[:, cs].astype(F32) * q_short
        wide[0, :, cs] = q_short
        wide[4, :, cs] = back_mix
        red[3:4, cs] = jnp.sum(back_mix * wide[3, :, cs], axis=0, keepdims=True)
        to_pieces(2, cb, back_mix)
    spread(2)

    def transform(slot):
        tmp[...] = dst[slot].astype(F32).reshape(pieces * OWN, rows)
        cols = [tmp[pl.ds(c, pieces, stride=OWN), :] for c in range(OWN)]
        signal = jnp.concatenate(cols, axis=1).astype(BF16)
        part = jnp.dot(
            outf_ref[...],
            jnp.concatenate([signal, signal], axis=0),
            preferred_element_type=F32,
        )
        cos, sin = tcos_ref[...], tsin_ref[...]
        for c in range(OWN):
            re = part[:pieces, c * rows : (c + 1) * rows]
            im = part[pieces:, c * rows : (c + 1) * rows]
            here = slice(c * pieces, (c + 1) * pieces)
            bbuf[here, :rows] = (re * cos + im * sin).astype(BF16)
            bbuf[here, rows:] = (im * cos - re * sin).astype(BF16)
        spec[slot] = jnp.dot(bbuf[...], inf_ref[...], preferred_element_type=F32)

    def inverse(slot, left, right, conj):
        a_re, a_im = spec[left, :, :rows], spec[left, :, rows:]
        b_re, b_im = spec[right, :, :rows], spec[right, :, rows:]
        if conj:
            bbuf[:, :rows] = (a_re * b_re + a_im * b_im).astype(BF16)
            bbuf[:, rows:] = (a_re * b_im - a_im * b_re).astype(BF16)
        else:
            bbuf[:, :rows] = (a_re * b_re - a_im * b_im).astype(BF16)
            bbuf[:, rows:] = (a_re * b_im + a_im * b_re).astype(BF16)
        part = jnp.dot(bbuf[...], ini_ref[...], preferred_element_type=F32)
        cos, sin = tcos_ref[...], tsin_ref[...]
        cols = []
        for c in range(OWN):
            re = part[c * pieces : (c + 1) * pieces, :rows]
            im = part[c * pieces : (c + 1) * pieces, rows:]
            turned = [(re * cos - im * sin).astype(BF16), (im * cos + re * sin).astype(BF16)]
            cols.append(jnp.concatenate(turned, axis=0))
        turned = jnp.concatenate(cols, axis=1)
        out = jnp.dot(
            outi_ref[...],
            jnp.concatenate([turned, turned], axis=0),
            preferred_element_type=F32,
        )
        square = jnp.sum(out * out, axis=0, keepdims=True)
        for c in range(OWN):
            tmp[pl.ds(c, pieces, stride=OWN), :] = out[:, c * rows : (c + 1) * rows]
        src[slot] = tmp[...].reshape(pieces, OWN, rows).astype(BF16)
        return sum(square[:, c * rows : (c + 1) * rows] for c in range(OWN))

    arrived(0)
    transform(0)
    arrived(1)
    transform(1)
    inverse(3, 0, 1, False)
    spread(3)
    arrived(2)
    transform(2)
    inverse(4, 0, 2, True)
    spread(4)
    square = inverse(5, 1, 2, True)
    spread(5)

    red[4:8, :] = jnp.zeros((4, channels), F32)
    red[4:5, :rows] = square

    arrived(3)
    for cb, cs in enumerate(blocks):
        filtered = from_pieces(3, cb) + skip_ref[:, cs] * wide[3, :, cs]
        mixed_ref[:, cs] = (wide[0, :, cs] * filtered).astype(BF16)
        back[0, :rows, cs] = go_ref[:, cs].astype(F32) * filtered
    arrived(4)
    for cb, cs in enumerate(blocks):
        back_prod = from_pieces(4, cb) + skip_ref[:, cs] * wide[4, :, cs]
        back[1, :rows, cs] = back_prod * wide[2, :, cs]
        back[2, :rows, cs] = back_prod * wide[1, :, cs]
        for j in range(3):
            total = back[0, :rows, cs] * ext[0, 8 - j : 8 - j + rows, cs]
            for i in range(1, 3):
                total = total + back[i, :rows, cs] * ext[i, 8 - j : 8 - j + rows, cs]
            red[j : j + 1, cs] = jnp.sum(total, axis=0, keepdims=True)

    @pl.loop(1, group_a)
    def _(step):
        peer = lax.rem(my_a + step, group_a)
        pltpu.make_async_remote_copy(
            red,
            red1.at[my_a],
            ssem.at[SUM1],
            rsem.at[SUM1],
            device_id=(ctx_of(peer, my_b), ch),
            device_id_type=MESH,
        ).start()

    red1[my_a] = red[...]

    for i in range(3):
        tsrc[2 * i : 2 * i + 2, :] = back[i, 0:2, :]
    tsrc[6:8, :] = jnp.zeros((2, channels), F32)
    tail = pltpu.make_async_remote_copy(
        tsrc,
        tdst,
        ssem.at[TAIL],
        rsem.at[TAIL],
        device_id=(lax.rem(me + pieces - 1, pieces), ch),
        device_id_type=MESH,
    )
    tail.start()

    def wait_many(ref, count, sem):
        view = ref.at[pl.ds(0, count)]
        pltpu.make_async_copy(view, view, sem).wait()

    wait_many(red1, group_a - 1, rsem.at[SUM1])
    wait_many(red1, group_a - 1, ssem.at[SUM1])
    total = red1[0]
    for i in range(1, group_a):
        total = total + red1[i]
    red[...] = total

    @pl.loop(1, group_b)
    def _(step):
        peer = lax.rem(my_b + step, group_b)
        pltpu.make_async_remote_copy(
            red,
            red2.at[my_b],
            ssem.at[SUM2],
            rsem.at[SUM2],
            device_id=(ctx_of(my_a, peer), ch),
            device_id_type=MESH,
        ).start()

    red2[my_b] = red[...]

    tail.wait_recv()
    for i, ref in enumerate((gq_ref, gk_ref, gv_ref)):
        tail_rows = tdst[2 * i : 2 * i + 2, :]
        back[i, rows : rows + 2, :] = jnp.where(
            me < pieces - 1, tail_rows, jnp.zeros_like(tail_rows)
        )
        for cs in blocks:
            total = taps_at(0, cs) * back[i, 0:rows, cs]
            for j in range(1, 3):
                total = total + taps_at(j, cs) * back[i, j : j + rows, cs]
            ref[:, cs] = total.astype(BF16)

    wait_many(red2, group_b - 1, rsem.at[SUM2])
    wait_many(red2, group_b - 1, ssem.at[SUM2])
    sums = red2[0]
    for i in range(1, group_b):
        sums = sums + red2[i]
    row = lax.broadcasted_iota(jnp.int32, sums.shape, 0)
    squares = jnp.where(row < 4, sums * sums, sums)
    nrm[...] = jnp.broadcast_to(jnp.sum(squares, keepdims=True), nrm.shape)

    @pl.loop(1, chs)
    def _(step):
        peer = lax.rem(ch + step, chs)
        pltpu.make_async_remote_copy(
            nrm,
            nrmd.at[ch],
            ssem.at[NORM],
            rsem.at[NORM],
            device_id=(me, peer),
            device_id_type=MESH,
        ).start()

    nrmd[ch] = nrm[...]

    arrived(5)
    for cb, cs in enumerate(blocks):
        gkern_ref[:, cs] = from_pieces(5, cb)

    wait_many(nrmd, chs - 1, rsem.at[NORM])
    wait_many(nrmd, chs - 1, ssem.at[NORM])
    norm_sq = nrmd[0]
    for i in range(1, chs):
        norm_sq = norm_sq + nrmd[i]
    factor = limit / jnp.maximum(jnp.sqrt(norm_sq), limit)
    factor = factor[0:1, 0:1]
    small_ref[...] = factor * sums
    gkern_ref[...] = factor * gkern_ref[...]

    halo.wait_send()
    tail.wait_send()
    for slot in range(6):
        view = src.at[slot, pl.ds(0, pieces - 1)]
        pltpu.make_async_copy(view, view, ssem.at[KERN + slot]).wait()


def body(sizes, q_in, k_in, v_in, grad_out, short_filter, kernel, skip):
    pieces, chs = sizes
    rows, channels = q_in.shape
    group_a = group_b = math.isqrt(pieces)
    limit = math.sqrt(float(pieces * rows * channels * chs))
    consts = [jnp.asarray(table) for table in tables(pieces, rows)]
    wide = jax.ShapeDtypeStruct((rows, channels), BF16)
    vmem = pl.BlockSpec(memory_space=pltpu.VMEM)
    mixed, grad_q, grad_k, grad_v, grad_kernel, small = pl.pallas_call(
        functools.partial(mixer_kernel, (pieces, group_a, group_b, chs), limit),
        out_shape=[
            wide,
            wide,
            wide,
            wide,
            jax.ShapeDtypeStruct((rows, channels), F32),
            jax.ShapeDtypeStruct((8, channels), F32),
        ],
        in_specs=[vmem] * 13,
        out_specs=[vmem] * 6,
        scratch_shapes=[
            pltpu.VMEM((6, pieces, OWN, rows), BF16),
            pltpu.VMEM((6, pieces, OWN, rows), BF16),
            pltpu.VMEM((3, rows + 8, channels), F32),
            pltpu.VMEM((5, rows, channels), F32),
            pltpu.VMEM((3, rows + 8, channels), F32),
            pltpu.VMEM((8, channels), F32),
            pltpu.VMEM((8, channels), F32),
            pltpu.VMEM((8, channels), F32),
            pltpu.VMEM((8, channels), F32),
            pltpu.VMEM((pieces * OWN, rows), F32),
            pltpu.VMEM((pieces * OWN, 2 * rows), BF16),
            pltpu.VMEM((3, pieces * OWN, 2 * rows), F32),
            pltpu.VMEM((8, channels), F32),
            pltpu.VMEM((group_a, 8, channels), F32),
            pltpu.VMEM((group_b, 8, channels), F32),
            pltpu.VMEM((8, LANES), F32),
            pltpu.VMEM((chs, 8, LANES), F32),
            pltpu.SemaphoreType.DMA((11,)),
            pltpu.SemaphoreType.DMA((11,)),
        ],
        compiler_params=pltpu.CompilerParams(
            collective_id=0, has_side_effects=True, vmem_limit_bytes=40 << 20
        ),
        name="mixer",
    )(q_in, k_in, v_in, grad_out, kernel, short_filter, skip[None, :], *consts)
    return mixed, grad_q, grad_k, grad_v, small[:3], small[3], grad_kernel


def solution(mesh):
    whole = P("ctx", "ch")
    return jax.shard_map(
        functools.partial(body, (mesh.shape["ctx"], mesh.shape["ch"])),
        mesh=mesh,
        in_specs=(whole, whole, whole, whole, P(None, "ch"), whole, P("ch")),
        out_specs=(whole, whole, whole, whole, P(None, "ch"), P("ch"), whole),
        check_vma=False,
    )
```

```python
import functools
import math

import jax
import jax.numpy as jnp
import numpy as np
from jax import lax
from jax.experimental import pallas as pl
from jax.experimental.pallas import tpu as pltpu
from jax.sharding import PartitionSpec as P

MESH = pl.DeviceIdType.MESH
F32 = jnp.float32
BF16 = jnp.bfloat16
LANES = 128
OWN = 8
HALO, KERN, PROD, BACK, CONV, CORR, LAG, TAIL, SUM1, SUM2, SUM3, NORM = range(12)


def split_table(table):
    high = table.astype(np.float32).astype(jnp.bfloat16)
    low = (table - high.astype(np.float64)).astype(np.float32).astype(jnp.bfloat16)
    return high, low


def tables(blocks, rows):
    length = blocks * rows
    outer = 2.0 * np.pi * np.outer(np.arange(blocks) + 0.25, np.arange(blocks)) / blocks
    twist = 2.0 * np.pi * np.outer(np.arange(blocks) + 0.25, np.arange(rows)) / length
    inner = 2.0 * np.pi * (np.outer(np.arange(rows), np.arange(rows)) % rows) / rows
    out_f = np.concatenate([np.cos(outer), -np.sin(outer)], axis=0)
    out_i = np.concatenate([np.cos(outer.T), -np.sin(outer.T)], axis=1) / length
    cos, sin = np.cos(inner), np.sin(inner)
    in_f = np.block([[cos, -sin], [sin, cos]])
    in_i = np.block([[cos, sin], [-sin, cos]])
    return (
        np.concatenate(split_table(out_f), axis=1),
        np.concatenate(split_table(out_i), axis=1),
        split_table(in_f)[0],
        split_table(in_i)[0],
        np.cos(twist).astype(np.float32),
        np.sin(twist).astype(np.float32),
    )


def mixer_kernel(
    dims,
    limit,
    *refs,
):
    inputs, refs = refs[:13], refs[13:]
    outputs, refs = refs[:7], refs[7:]
    loaded, refs = refs[:13], refs[13:]
    (
    kern_ref,
    k_ref,
    v_ref,
    q_ref,
    go_ref,
    taps_ref,
    outf_ref,
    inf_ref,
    tcos_ref,
    tsin_ref,
    outi_ref,
    ini_ref,
    skip_ref,
    ) = loaded
    ready, refs = refs[:7], refs[7:]
    (
    mixed_ref,
    gq_ref,
    gk_ref,
    gv_ref,
    lag_ref,
    small_ref,
    factor_ref,
    ) = ready
    (
    src,
    dst,
    ext,
    wide,
    back,
    hsrc,
    hdst,
    tsrc,
    tdst,
    tmp,
    bbuf,
    spec,
    part1,
    red1,
    part2,
    red2,
    part3,
    red3,
    nrm,
    nrmd,
    ssem,
    rsem,
    isem,
    osem,
    ) = refs
    pieces, group_a, group_b, chs = dims
    rows, channels = q_ref.shape
    me = lax.axis_index("ctx")
    ch = lax.axis_index("ch")
    my_a = me // (2 * group_b) * 2 + me % 2
    my_b = me // 2 % group_b

    def ctx_of(a, b):
        return (a // 2 * group_b + b) * 2 + a % 2

    loads = [
        pltpu.make_async_copy(far, near, isem.at[i])
        for i, (far, near) in enumerate(zip(inputs, loaded))
    ]
    for load in loads:
        load.start()

    barrier = pltpu.get_barrier_semaphore()

    @pl.loop(1, pieces, unroll=9)
    def _(step):
        peer = lax.rem(me + step, pieces)
        pl.semaphore_signal(barrier, inc=1, device_id=(peer, ch), device_id_type=MESH)

    @pl.loop(1, chs)
    def _(step):
        peer = lax.rem(ch + step, chs)
        pl.semaphore_signal(barrier, inc=1, device_id=(me, peer), device_id_type=MESH)

    def spread(slot):
        @pl.loop(1, pieces, unroll=9)
        def _(step):
            peer = lax.rem(me + step, pieces)
            pltpu.make_async_remote_copy(
                src.at[slot, peer],
                dst.at[slot, me],
                ssem.at[KERN + slot],
                rsem.at[KERN + slot],
                device_id=(peer, ch),
                device_id_type=MESH,
            ).start()

        dst[slot, me] = src[slot, me]

    def arrived(slot):
        view = dst.at[slot, pl.ds(0, pieces - 1)]
        pltpu.make_async_copy(view, view, rsem.at[KERN + slot]).wait()

    def to_pieces(slot, cb, block):
        per = LANES // OWN
        src[slot, cb * per : (cb + 1) * per] = block.T.reshape(per, OWN, rows).astype(BF16)

    def from_pieces(slot, cb):
        per = LANES // OWN
        block = dst[slot, cb * per : (cb + 1) * per].astype(F32)
        return block.reshape(LANES, rows).T

    blocks = [slice(cb * LANES, (cb + 1) * LANES) for cb in range(channels // LANES)]

    stores = [
        pltpu.make_async_copy(near, far, osem.at[i])
        for i, (near, far) in enumerate(zip(ready, outputs))
    ]

    loads[0].wait()
    for cb, cs in enumerate(blocks):
        to_pieces(0, cb, kern_ref[:, cs])
    for i, (ref, order) in enumerate(((q_ref, 3), (k_ref, 1), (v_ref, 2))):
        loads[order].wait()
        ext[i, 8 : 8 + rows, :] = ref[...].astype(F32)
        hsrc[2 * i : 2 * i + 2, :] = ext[i, 6 + rows : 8 + rows, :]
    hsrc[6:8, :] = jnp.zeros((2, channels), F32)

    pl.semaphore_wait(barrier, pieces - 1 + chs - 1)

    halo = pltpu.make_async_remote_copy(
        hsrc,
        hdst,
        ssem.at[HALO],
        rsem.at[HALO],
        device_id=(lax.rem(me + 1, pieces), ch),
        device_id_type=MESH,
    )
    halo.start()
    spread(0)
    for load in loads[4:]:
        load.wait()
    halo.wait_recv()

    def taps_at(j, cs):
        return taps_ref[j : j + 1, cs]

    def short(i, cs):
        total = taps_at(0, cs) * ext[i, 8 : 8 + rows, cs]
        for j in range(1, 3):
            total = total + taps_at(j, cs) * ext[i, 8 - j : 8 - j + rows, cs]
        return total

    for i in range(3):
        halo_rows = hdst[2 * i : 2 * i + 2, :]
        ext[i, 6:8, :] = jnp.where(me > 0, halo_rows, jnp.zeros_like(halo_rows))
    for cb, cs in enumerate(blocks):
        k_short = short(1, cs)
        v_short = short(2, cs)
        product = (k_short * v_short).astype(BF16).astype(F32)
        wide[1, :, cs] = k_short
        wide[2, :, cs] = v_short
        wide[3, :, cs] = product
        to_pieces(1, cb, product)
    spread(1)
    for cb, cs in enumerate(blocks):
        q_short = short(0, cs)
        back_mix = go_ref[:, cs].astype(F32) * q_short
        wide[0, :, cs] = q_short
        wide[4, :, cs] = back_mix
        part1[2 * cb + 1, 1:2, :] = jnp.sum(back_mix * wide[3, :, cs], axis=0, keepdims=True)
        to_pieces(2, cb, back_mix)
    spread(2)

    def transform(slot):
        tmp[...] = dst[slot].astype(F32).reshape(pieces * OWN, rows)
        cols = [tmp[pl.ds(c, pieces, stride=OWN), :] for c in range(OWN)]
        signal = jnp.concatenate(cols, axis=1).astype(BF16)
        part = jnp.dot(
            outf_ref[...],
            jnp.concatenate([signal, signal], axis=0),
            preferred_element_type=F32,
        )
        cos, sin = tcos_ref[...], tsin_ref[...]
        for c in range(OWN):
            re = part[:pieces, c * rows : (c + 1) * rows]
            im = part[pieces:, c * rows : (c + 1) * rows]
            here = slice(c * pieces, (c + 1) * pieces)
            bbuf[here, :rows] = (re * cos + im * sin).astype(BF16)
            bbuf[here, rows:] = (im * cos - re * sin).astype(BF16)
        spec[slot] = jnp.dot(bbuf[...], inf_ref[...], preferred_element_type=F32)

    def inverse(slot, left, right, conj):
        a_re, a_im = spec[left, :, :rows], spec[left, :, rows:]
        b_re, b_im = spec[right, :, :rows], spec[right, :, rows:]
        if conj:
            bbuf[:, :rows] = (a_re * b_re + a_im * b_im).astype(BF16)
            bbuf[:, rows:] = (a_re * b_im - a_im * b_re).astype(BF16)
        else:
            bbuf[:, :rows] = (a_re * b_re - a_im * b_im).astype(BF16)
            bbuf[:, rows:] = (a_re * b_im + a_im * b_re).astype(BF16)
        part = jnp.dot(bbuf[...], ini_ref[...], preferred_element_type=F32)
        cos, sin = tcos_ref[...], tsin_ref[...]
        cols = []
        for c in range(OWN):
            re = part[c * pieces : (c + 1) * pieces, :rows]
            im = part[c * pieces : (c + 1) * pieces, rows:]
            turned = [(re * cos - im * sin).astype(BF16), (im * cos + re * sin).astype(BF16)]
            cols.append(jnp.concatenate(turned, axis=0))
        turned = jnp.concatenate(cols, axis=1)
        out = jnp.dot(
            outi_ref[...],
            jnp.concatenate([turned, turned], axis=0),
            preferred_element_type=F32,
        )
        square = jnp.sum(out * out, axis=0, keepdims=True)
        for c in range(OWN):
            tmp[pl.ds(c, pieces, stride=OWN), :] = out[:, c * rows : (c + 1) * rows]
        src[slot] = tmp[...].reshape(pieces, OWN, rows).astype(BF16)
        return sum(square[:, c * rows : (c + 1) * rows] for c in range(OWN))

    arrived(0)
    transform(0)
    arrived(1)
    transform(1)
    inverse(3, 0, 1, False)
    spread(3)
    arrived(2)
    transform(2)
    inverse(4, 0, 2, True)
    spread(4)
    square = inverse(5, 1, 2, True)
    spread(5)

    part2[2:3, :] = square
    part2[3:4, :] = jnp.zeros_like(square)

    arrived(3)
    for cb, cs in enumerate(blocks):
        filtered = from_pieces(3, cb) + skip_ref[:, cs] * wide[3, :, cs]
        mixed_ref[:, cs] = (wide[0, :, cs] * filtered).astype(BF16)
        back[0, :rows, cs] = go_ref[:, cs].astype(F32) * filtered
    stores[0].start()
    arrived(4)
    for cb, cs in enumerate(blocks):
        back_prod = from_pieces(4, cb) + skip_ref[:, cs] * wide[4, :, cs]
        back[1, :rows, cs] = back_prod * wide[2, :, cs]
        back[2, :rows, cs] = back_prod * wide[1, :, cs]
        for j in range(3):
            total = back[0, :rows, cs] * ext[0, 8 - j : 8 - j + rows, cs]
            for i in range(1, 3):
                total = total + back[i, :rows, cs] * ext[i, 8 - j : 8 - j + rows, cs]
            here = 2 * cb + j // 2
            part1[here, j % 2 : j % 2 + 1, :] = jnp.sum(total, axis=0, keepdims=True)

    def exchange(source, slots, mine, size, sem, device_of, own):
        @pl.loop(1, size, unroll=True)
        def _(step):
            peer = lax.rem(mine + step, size)
            pltpu.make_async_remote_copy(
                source(peer),
                slots.at[mine],
                ssem.at[sem],
                rsem.at[sem],
                device_id=device_of(peer),
                device_id_type=MESH,
            ).start()

        slots[mine] = own()

    def wait_many(slots, size, sem):
        view = slots.at[pl.ds(0, size - 1)]
        pltpu.make_async_copy(view, view, sem).wait()

    def total_of(slots, size, sem):
        wait_many(slots, size, rsem.at[sem])
        total = slots[0]
        for i in range(1, size):
            total = total + slots[i]
        return total

    def along_a(peer):
        return (ctx_of(peer, my_b), ch)

    exchange(
        lambda peer: part1.at[peer], red1, my_a, group_a, SUM1, along_a, lambda: part1[my_a]
    )

    for i in range(3):
        tsrc[2 * i : 2 * i + 2, :] = back[i, 0:2, :]
    tsrc[6:8, :] = jnp.zeros((2, channels), F32)
    tail = pltpu.make_async_remote_copy(
        tsrc,
        tdst,
        ssem.at[TAIL],
        rsem.at[TAIL],
        device_id=(lax.rem(me + pieces - 1, pieces), ch),
        device_id_type=MESH,
    )
    tail.start()

    part2[0:2, :] = total_of(red1, group_a, SUM1)
    exchange(
        lambda peer: part2,
        red2,
        my_b,
        group_b,
        SUM2,
        lambda peer: (ctx_of(my_a, peer), ch),
        lambda: part2[...],
    )

    tail.wait_recv()
    for i, ref in enumerate((gq_ref, gk_ref, gv_ref)):
        tail_rows = tdst[2 * i : 2 * i + 2, :]
        back[i, rows : rows + 2, :] = jnp.where(
            me < pieces - 1, tail_rows, jnp.zeros_like(tail_rows)
        )
        for cs in blocks:
            total = taps_at(0, cs) * back[i, 0:rows, cs]
            for j in range(1, 3):
                total = total + taps_at(j, cs) * back[i, j : j + rows, cs]
            ref[:, cs] = total.astype(BF16)
        stores[1 + i].start()

    part3[...] = total_of(red2, group_b, SUM2)
    exchange(lambda peer: part3, red3, my_a, group_a, SUM3, along_a, lambda: part3[...])

    arrived(5)
    for cb, cs in enumerate(blocks):
        lag_ref[:, cs] = from_pieces(5, cb).astype(BF16)
    stores[4].start()

    wait_many(red3, group_a, rsem.at[SUM3])
    row = lax.broadcasted_iota(jnp.int32, part3.shape, 0)
    square = jnp.zeros(part3.shape, F32)
    for a in range(group_a):
        piece = red3[a]
        square = square + jnp.where(row < 2, piece * piece, piece)
        first = 2 * (a % 2)
        small_ref[first : first + 2, a // 2 * LANES : (a // 2 + 1) * LANES] = piece[0:2]
    nrm[...] = jnp.broadcast_to(jnp.sum(square, keepdims=True), nrm.shape)
    exchange(
        lambda peer: nrm, nrmd, ch, chs, NORM, lambda peer: (me, peer), lambda: nrm[...]
    )
    stores[5].start()
    norm_sq = total_of(nrmd, chs, NORM)
    factor_ref[...] = limit / jnp.maximum(jnp.sqrt(norm_sq), limit)
    stores[6].start()

    wait_many(red1, group_a, ssem.at[SUM1])
    wait_many(red2, group_b, ssem.at[SUM2])
    wait_many(red3, group_a, ssem.at[SUM3])
    wait_many(nrmd, chs, ssem.at[NORM])
    halo.wait_send()
    tail.wait_send()
    for slot in range(6):
        view = src.at[slot, pl.ds(0, pieces - 1)]
        pltpu.make_async_copy(view, view, ssem.at[KERN + slot]).wait()
    for store in stores:
        store.wait()


def store_kernel(*refs):
    parts, outs, near, refs = refs[:7], refs[7:14], refs[14:21], refs[21:]
    kern, short, skip, isem, osem = refs
    lag_ref, small_ref, factor_ref = near[4:]
    loads = [pltpu.make_async_copy(a, b, isem.at[i]) for i, (a, b) in enumerate(zip(parts, near))]
    order = (6, 4, 5, 0, 1, 2, 3)
    for i in order:
        loads[i].start()
    ready = (*near[:4], kern, short, skip)
    stores = [pltpu.make_async_copy(a, b, osem.at[i]) for i, (a, b) in enumerate(zip(ready, outs))]
    for i in order[:3]:
        loads[i].wait()
    factor = factor_ref[0:1, 0:1]
    kern[...] = factor * lag_ref[...].astype(F32)
    stores[4].start()
    short[...] = factor * small_ref[0:3, :]
    skip[...] = (factor * small_ref[3:4, :]).reshape(skip.shape)
    stores[5].start()
    stores[6].start()
    for i in range(4):
        loads[i].wait()
        stores[i].start()
    for store in stores:
        store.wait()


def body(sizes, q_in, k_in, v_in, grad_out, short_filter, kernel, skip):
    pieces, chs = sizes
    rows, channels = q_in.shape
    group_a = group_b = math.isqrt(pieces)
    limit = math.sqrt(float(pieces * rows * channels * chs))
    consts = [jnp.asarray(table) for table in tables(pieces, rows)]
    wide = jax.ShapeDtypeStruct((rows, channels), BF16)
    far = pl.BlockSpec(memory_space=pltpu.HBM)
    operands = [kernel, k_in, v_in, q_in, grad_out, short_filter]
    operands += [consts[0], consts[2], consts[4], consts[5], consts[1], consts[3]]
    operands.append(skip[None, :])
    f32_wide = jax.ShapeDtypeStruct((rows, channels), F32)
    results = [
        wide,
        wide,
        wide,
        wide,
        wide,
        jax.ShapeDtypeStruct((4, channels), F32),
        jax.ShapeDtypeStruct((1, LANES), F32),
    ]
    parts = pl.pallas_call(
        functools.partial(mixer_kernel, (pieces, group_a, group_b, chs), limit),
        out_shape=results,
        in_specs=[far] * 13,
        out_specs=[far] * 7,
        scratch_shapes=[
            *(pltpu.VMEM(x.shape, x.dtype) for x in operands),
            *(pltpu.VMEM(x.shape, x.dtype) for x in results),
            pltpu.VMEM((6, pieces, OWN, rows), BF16),
            pltpu.VMEM((6, pieces, OWN, rows), BF16),
            pltpu.VMEM((3, rows + 8, channels), F32),
            pltpu.VMEM((5, rows, channels), F32),
            pltpu.VMEM((3, rows + 8, channels), F32),
            *(pltpu.VMEM((8, channels), F32) for _ in range(4)),
            pltpu.VMEM((pieces * OWN, rows), F32),
            pltpu.VMEM((pieces * OWN, 2 * rows), BF16),
            pltpu.VMEM((3, pieces * OWN, 2 * rows), F32),
            pltpu.VMEM((group_a, 2, LANES), F32),
            pltpu.VMEM((group_a, 2, LANES), F32),
            pltpu.VMEM((4, LANES), F32),
            pltpu.VMEM((group_b, 4, LANES), F32),
            pltpu.VMEM((4, LANES), F32),
            pltpu.VMEM((group_a, 4, LANES), F32),
            pltpu.VMEM((1, LANES), F32),
            pltpu.VMEM((chs, 1, LANES), F32),
            pltpu.SemaphoreType.DMA((12,)),
            pltpu.SemaphoreType.DMA((12,)),
            pltpu.SemaphoreType.DMA((13,)),
            pltpu.SemaphoreType.DMA((7,)),
        ],
        compiler_params=pltpu.CompilerParams(
            collective_id=0, has_side_effects=True, vmem_limit_bytes=63 << 20
        ),
        name="mixer",
    )(*operands)
    out = pl.pallas_call(
        store_kernel,
        out_shape=[
            wide,
            wide,
            wide,
            wide,
            f32_wide,
            jax.ShapeDtypeStruct((3, channels), F32),
            jax.ShapeDtypeStruct((channels,), F32),
        ],
        in_specs=[far] * 7,
        out_specs=[far] * 7,
        scratch_shapes=[
            *(pltpu.VMEM(x.shape, x.dtype) for x in results),
            pltpu.VMEM((rows, channels), F32),
            pltpu.VMEM((3, channels), F32),
            pltpu.VMEM((channels,), F32),
            pltpu.SemaphoreType.DMA((7,)),
            pltpu.SemaphoreType.DMA((7,)),
        ],
        compiler_params=pltpu.CompilerParams(vmem_limit_bytes=63 << 20),
        name="store",
    )(*parts)
    mixed, grad_q, grad_k, grad_v, grad_kernel, grad_short, grad_skip = out
    return mixed, grad_q, grad_k, grad_v, grad_short, grad_skip, grad_kernel


def solution(mesh):
    whole = P("ctx", "ch")
    return jax.shard_map(
        functools.partial(body, (mesh.shape["ctx"], mesh.shape["ch"])),
        mesh=mesh,
        in_specs=(whole, whole, whole, whole, P(None, "ch"), whole, P("ch")),
        out_specs=(whole, whole, whole, whole, P(None, "ch"), P("ch"), whole),
        check_vma=False,
    )
```

```python
import functools
import math

import jax
import jax.numpy as jnp
import numpy as np
from jax import lax
from jax.experimental import pallas as pl
from jax.experimental.pallas import tpu as pltpu
from jax.sharding import PartitionSpec as P

MESH = pl.DeviceIdType.MESH
F32 = jnp.float32
BF16 = jnp.bfloat16
LANES = 128
OWN = 8
HALO, KERN, PROD, BACK, CONV, CORR, LAG, TAIL, SUM1, SUM2, NORM = range(11)


def split_table(table):
    high = table.astype(np.float32).astype(jnp.bfloat16)
    low = (table - high.astype(np.float64)).astype(np.float32).astype(jnp.bfloat16)
    return high, low


def tables(blocks, rows):
    length = blocks * rows
    outer = 2.0 * np.pi * np.outer(np.arange(blocks) + 0.25, np.arange(blocks)) / blocks
    twist = 2.0 * np.pi * np.outer(np.arange(blocks) + 0.25, np.arange(rows)) / length
    inner = 2.0 * np.pi * (np.outer(np.arange(rows), np.arange(rows)) % rows) / rows
    out_f = np.concatenate([np.cos(outer), -np.sin(outer)], axis=0)
    out_i = np.concatenate([np.cos(outer.T), -np.sin(outer.T)], axis=1) / length
    cos, sin = np.cos(inner), np.sin(inner)
    in_f = np.block([[cos, -sin], [sin, cos]])
    in_i = np.block([[cos, sin], [-sin, cos]])
    return (
        np.concatenate(split_table(out_f), axis=1),
        np.concatenate(split_table(out_i), axis=1),
        split_table(in_f)[0],
        split_table(in_i)[0],
        np.cos(twist).astype(np.float32),
        np.sin(twist).astype(np.float32),
    )


def by_distance(size):
    return sorted(range(size), key=lambda k: -min(k, size - k))


def mixer_kernel(
    dims,
    limit,
    *refs,
):
    inputs, refs = refs[:13], refs[13:]
    outputs, refs = refs[:7], refs[7:]
    loaded, refs = refs[:13], refs[13:]
    (
    kern_ref,
    k_ref,
    v_ref,
    q_ref,
    go_ref,
    taps_ref,
    outf_ref,
    inf_ref,
    tcos_ref,
    tsin_ref,
    outi_ref,
    ini_ref,
    skip_ref,
    ) = loaded
    (
    mixed_ref,
    gq_ref,
    gk_ref,
    gv_ref,
    lag_ref,
    small_ref,
    factor_ref,
    ) = outputs
    (
    src,
    dst,
    ext,
    wide,
    back,
    hsrc,
    hdst,
    tsrc,
    tdst,
    tmp,
    bbuf,
    spec,
    part,
    red1,
    red2,
    nrm,
    nrmd,
    ssem,
    rsem,
    isem,
    ) = refs
    pieces, group_a, group_b, chs = dims
    rows, channels = q_ref.shape
    me = lax.axis_index("ctx")
    ch = lax.axis_index("ch")
    my_a = me // (2 * group_b) * 2 + me % 2
    my_b = me // 2 % group_b

    def ctx_of(a, b):
        return (a // 2 * group_b + b) * 2 + a % 2

    others = [k for k in by_distance(group_a) if k]
    corners = {k: ctx_of(lax.rem(my_a + k, group_a), 0) for k in range(group_a)}

    def each_peer(visit):
        @pl.loop(0, group_b - 1)
        def _(i):
            ahead = i // 2 * (1 - i % 2) - (i + 1) // 2 * (i % 2)
            b = lax.rem(my_b + group_b // 2 + ahead, group_b)
            for k in by_distance(group_a):
                visit(corners[k] + 2 * b)

        for k in others:
            visit(corners[k] + 2 * my_b)

    barrier = pltpu.get_barrier_semaphore()

    def greet(a, b):
        pl.semaphore_signal(barrier, inc=1, device_id=(a, b), device_id_type=MESH)

    each_peer(lambda peer: greet(peer, ch))
    for k in by_distance(chs):
        if k:
            greet(me, lax.rem(ch + k, chs))

    loads = [
        pltpu.make_async_copy(far, near, isem.at[i])
        for i, (far, near) in enumerate(zip(inputs, loaded))
    ]
    for load in loads:
        load.start()

    def spread(slot):
        def send(peer):
            pltpu.make_async_remote_copy(
                src.at[slot, peer],
                dst.at[slot, me],
                ssem.at[KERN + slot],
                rsem.at[KERN + slot],
                device_id=(peer, ch),
                device_id_type=MESH,
            ).start()

        each_peer(send)
        dst[slot, me] = src[slot, me]

    def arrived(slot):
        view = dst.at[slot, pl.ds(0, pieces - 1)]
        pltpu.make_async_copy(view, view, rsem.at[KERN + slot]).wait()

    def to_pieces(slot, cb, block):
        per = LANES // OWN
        src[slot, cb * per : (cb + 1) * per] = block.T.reshape(per, OWN, rows).astype(BF16)

    def from_pieces(slot, cb):
        per = LANES // OWN
        block = dst[slot, cb * per : (cb + 1) * per].astype(F32)
        return block.reshape(LANES, rows).T

    blocks = [slice(cb * LANES, (cb + 1) * LANES) for cb in range(channels // LANES)]

    loads[0].wait()
    for cb, cs in enumerate(blocks):
        to_pieces(0, cb, kern_ref[:, cs])
    for i, (ref, order) in enumerate(((q_ref, 3), (k_ref, 1), (v_ref, 2))):
        loads[order].wait()
        ext[i, 8 : 8 + rows, :] = ref[...].astype(F32)
        hsrc[2 * i : 2 * i + 2, :] = ext[i, 6 + rows : 8 + rows, :]
    hsrc[6:8, :] = jnp.zeros((2, channels), F32)

    pl.semaphore_wait(barrier, pieces - 1 + chs - 1)

    halo = pltpu.make_async_remote_copy(
        hsrc,
        hdst,
        ssem.at[HALO],
        rsem.at[HALO],
        device_id=(lax.rem(me + 1, pieces), ch),
        device_id_type=MESH,
    )
    halo.start()
    spread(0)
    for load in loads[4:]:
        load.wait()
    halo.wait_recv()

    def taps_at(j, cs):
        return taps_ref[j : j + 1, cs]

    def short(i, cs):
        total = taps_at(0, cs) * ext[i, 8 : 8 + rows, cs]
        for j in range(1, 3):
            total = total + taps_at(j, cs) * ext[i, 8 - j : 8 - j + rows, cs]
        return total

    for i in range(3):
        halo_rows = hdst[2 * i : 2 * i + 2, :]
        ext[i, 6:8, :] = jnp.where(me > 0, halo_rows, jnp.zeros_like(halo_rows))
    for cb, cs in enumerate(blocks):
        k_short = short(1, cs)
        v_short = short(2, cs)
        product = (k_short * v_short).astype(BF16).astype(F32)
        wide[1, :, cs] = k_short
        wide[2, :, cs] = v_short
        wide[3, :, cs] = product
        to_pieces(1, cb, product)
    spread(1)
    for cb, cs in enumerate(blocks):
        q_short = short(0, cs)
        back_mix = go_ref[:, cs].astype(F32) * q_short
        wide[0, :, cs] = q_short
        wide[4, :, cs] = back_mix
        part[3:4, cs] = jnp.sum(back_mix * wide[3, :, cs], axis=0, keepdims=True)
        to_pieces(2, cb, back_mix)
    spread(2)

    def transform(slot):
        tmp[...] = dst[slot].astype(F32).reshape(pieces * OWN, rows)
        cols = [tmp[pl.ds(c, pieces, stride=OWN), :] for c in range(OWN)]
        signal = jnp.concatenate(cols, axis=1).astype(BF16)
        part = jnp.dot(
            outf_ref[...],
            jnp.concatenate([signal, signal], axis=0),
            preferred_element_type=F32,
        )
        cos, sin = tcos_ref[...], tsin_ref[...]
        for c in range(OWN):
            re = part[:pieces, c * rows : (c + 1) * rows]
            im = part[pieces:, c * rows : (c + 1) * rows]
            here = slice(c * pieces, (c + 1) * pieces)
            bbuf[here, :rows] = (re * cos + im * sin).astype(BF16)
            bbuf[here, rows:] = (im * cos - re * sin).astype(BF16)
        spec[slot] = jnp.dot(bbuf[...], inf_ref[...], preferred_element_type=F32)

    def inverse(slot, left, right, conj):
        a_re, a_im = spec[left, :, :rows], spec[left, :, rows:]
        b_re, b_im = spec[right, :, :rows], spec[right, :, rows:]
        if conj:
            bbuf[:, :rows] = (a_re * b_re + a_im * b_im).astype(BF16)
            bbuf[:, rows:] = (a_re * b_im - a_im * b_re).astype(BF16)
        else:
            bbuf[:, :rows] = (a_re * b_re - a_im * b_im).astype(BF16)
            bbuf[:, rows:] = (a_re * b_im + a_im * b_re).astype(BF16)
        part = jnp.dot(bbuf[...], ini_ref[...], preferred_element_type=F32)
        cos, sin = tcos_ref[...], tsin_ref[...]
        cols = []
        for c in range(OWN):
            re = part[c * pieces : (c + 1) * pieces, :rows]
            im = part[c * pieces : (c + 1) * pieces, rows:]
            turned = [(re * cos - im * sin).astype(BF16), (im * cos + re * sin).astype(BF16)]
            cols.append(jnp.concatenate(turned, axis=0))
        turned = jnp.concatenate(cols, axis=1)
        out = jnp.dot(
            outi_ref[...],
            jnp.concatenate([turned, turned], axis=0),
            preferred_element_type=F32,
        )
        square = jnp.sum(out * out, axis=0, keepdims=True)
        for c in range(OWN):
            tmp[pl.ds(c, pieces, stride=OWN), :] = out[:, c * rows : (c + 1) * rows]
        src[slot] = tmp[...].reshape(pieces, OWN, rows).astype(BF16)
        return sum(square[:, c * rows : (c + 1) * rows] for c in range(OWN))

    arrived(0)
    transform(0)
    arrived(1)
    transform(1)
    inverse(3, 0, 1, False)
    spread(3)
    arrived(2)
    transform(2)
    inverse(4, 0, 2, True)
    spread(4)
    square = inverse(5, 1, 2, True)
    spread(5)

    part[:, channels:] = jnp.zeros((4, LANES), F32)
    part[0:1, channels:] = square

    arrived(3)
    for cb, cs in enumerate(blocks):
        filtered = from_pieces(3, cb) + skip_ref[:, cs] * wide[3, :, cs]
        mixed_ref[:, cs] = (wide[0, :, cs] * filtered).astype(BF16)
        back[0, :rows, cs] = go_ref[:, cs].astype(F32) * filtered
    arrived(4)
    for cb, cs in enumerate(blocks):
        back_prod = from_pieces(4, cb) + skip_ref[:, cs] * wide[4, :, cs]
        back[1, :rows, cs] = back_prod * wide[2, :, cs]
        back[2, :rows, cs] = back_prod * wide[1, :, cs]
        for j in range(3):
            total = back[0, :rows, cs] * ext[0, 8 - j : 8 - j + rows, cs]
            for i in range(1, 3):
                total = total + back[i, :rows, cs] * ext[i, 8 - j : 8 - j + rows, cs]
            part[j : j + 1, cs] = jnp.sum(total, axis=0, keepdims=True)

    def exchange(source, slots, mine, size, sem, device_of):
        for k in by_distance(size):
            if k:
                pltpu.make_async_remote_copy(
                    source,
                    slots.at[mine],
                    ssem.at[sem],
                    rsem.at[sem],
                    device_id=device_of(lax.rem(mine + k, size)),
                    device_id_type=MESH,
                ).start()
        slots[mine] = source[...]

    def wait_many(slots, size, sem):
        view = slots.at[pl.ds(0, size - 1)]
        pltpu.make_async_copy(view, view, sem).wait()

    def total_of(slots, size, sem):
        wait_many(slots, size, rsem.at[sem])
        total = slots[0]
        for i in range(1, size):
            total = total + slots[i]
        return total

    exchange(part, red1, my_a, group_a, SUM1, lambda peer: (ctx_of(peer, my_b), ch))

    for i in range(3):
        tsrc[2 * i : 2 * i + 2, :] = back[i, 0:2, :]
    tsrc[6:8, :] = jnp.zeros((2, channels), F32)
    tail = pltpu.make_async_remote_copy(
        tsrc,
        tdst,
        ssem.at[TAIL],
        rsem.at[TAIL],
        device_id=(lax.rem(me + pieces - 1, pieces), ch),
        device_id_type=MESH,
    )
    tail.start()

    sums = total_of(red1, group_a, SUM1)
    wait_many(red1, group_a, ssem.at[SUM1])
    part[...] = sums
    exchange(part, red2, my_b, group_b, SUM2, lambda peer: (ctx_of(my_a, peer), ch))

    tail.wait_recv()
    for i, ref in enumerate((gq_ref, gk_ref, gv_ref)):
        tail_rows = tdst[2 * i : 2 * i + 2, :]
        back[i, rows : rows + 2, :] = jnp.where(
            me < pieces - 1, tail_rows, jnp.zeros_like(tail_rows)
        )
        for cs in blocks:
            total = taps_at(0, cs) * back[i, 0:rows, cs]
            for j in range(1, 3):
                total = total + taps_at(j, cs) * back[i, j : j + rows, cs]
            ref[:, cs] = total.astype(BF16)

    sums = total_of(red2, group_b, SUM2)
    squares = sums[:, :channels] * sums[:, :channels]
    square = jnp.sum(squares, keepdims=True) + jnp.sum(sums[:, channels:], keepdims=True)
    nrm[...] = jnp.broadcast_to(square, nrm.shape)
    exchange(nrm, nrmd, ch, chs, NORM, lambda peer: (me, peer))
    small_ref[...] = sums[:, :channels]

    arrived(5)
    for cb, cs in enumerate(blocks):
        lag_ref[:, cs] = from_pieces(5, cb)

    norm_sq = total_of(nrmd, chs, NORM)
    factor_ref[...] = limit / jnp.maximum(jnp.sqrt(norm_sq), limit)

    wait_many(red2, group_b, ssem.at[SUM2])
    wait_many(nrmd, chs, ssem.at[NORM])
    halo.wait_send()
    tail.wait_send()
    for slot in range(6):
        view = src.at[slot, pl.ds(0, pieces - 1)]
        pltpu.make_async_copy(view, view, ssem.at[KERN + slot]).wait()


def store_kernel(*refs):
    near, far, (kern, short, skip, sem) = refs[:7], refs[7:14], refs[14:]
    lag_ref, small_ref, factor_ref = near[4:]
    copies = [pltpu.make_async_copy(a, b, sem.at[i]) for i, (a, b) in enumerate(zip(near[:4], far))]
    for copy in copies:
        copy.start()
    factor = factor_ref[0:1, 0:1]
    step = kern.shape[0] // 4
    for i in range(4):
        here = pl.ds(i * step, step)
        kern[here, :] = factor * lag_ref[here, :]
        copies.append(pltpu.make_async_copy(kern.at[here], far[4].at[here], sem.at[4 + i]))
        copies[-1].start()
    short[...] = factor * small_ref[0:3, :]
    skip[...] = (factor * small_ref[3:4, :]).reshape(skip.shape)
    for i, (a, b) in enumerate(((short, far[5]), (skip, far[6]))):
        copies.append(pltpu.make_async_copy(a, b, sem.at[8 + i]))
        copies[-1].start()
    for copy in copies:
        copy.wait()


def body(sizes, q_in, k_in, v_in, grad_out, short_filter, kernel, skip):
    pieces, chs = sizes
    rows, channels = q_in.shape
    group_a = group_b = math.isqrt(pieces)
    limit = math.sqrt(float(pieces * rows * channels * chs))
    consts = [jnp.asarray(table) for table in tables(pieces, rows)]
    wide = jax.ShapeDtypeStruct((rows, channels), BF16)
    far = pl.BlockSpec(memory_space=pltpu.HBM)
    near = pl.BlockSpec(memory_space=pltpu.VMEM)
    operands = [kernel, k_in, v_in, q_in, grad_out, short_filter]
    operands += [consts[0], consts[2], consts[4], consts[5], consts[1], consts[3]]
    operands.append(skip[None, :])
    f32_wide = jax.ShapeDtypeStruct((rows, channels), F32)
    results = [
        wide,
        wide,
        wide,
        wide,
        f32_wide,
        jax.ShapeDtypeStruct((4, channels), F32),
        jax.ShapeDtypeStruct((1, LANES), F32),
    ]
    parts = pl.pallas_call(
        functools.partial(mixer_kernel, (pieces, group_a, group_b, chs), limit),
        out_shape=results,
        in_specs=[far] * 13,
        out_specs=[near] * 7,
        scratch_shapes=[
            *(pltpu.VMEM(x.shape, x.dtype) for x in operands),
            pltpu.VMEM((6, pieces, OWN, rows), BF16),
            pltpu.VMEM((6, pieces, OWN, rows), BF16),
            pltpu.VMEM((3, rows + 8, channels), F32),
            pltpu.VMEM((5, rows, channels), F32),
            pltpu.VMEM((3, rows + 8, channels), F32),
            *(pltpu.VMEM((8, channels), F32) for _ in range(4)),
            pltpu.VMEM((pieces * OWN, rows), F32),
            pltpu.VMEM((pieces * OWN, 2 * rows), BF16),
            pltpu.VMEM((3, pieces * OWN, 2 * rows), F32),
            pltpu.VMEM((4, channels + LANES), F32),
            pltpu.VMEM((group_a, 4, channels + LANES), F32),
            pltpu.VMEM((group_b, 4, channels + LANES), F32),
            pltpu.VMEM((1, LANES), F32),
            pltpu.VMEM((chs, 1, LANES), F32),
            pltpu.SemaphoreType.DMA((11,)),
            pltpu.SemaphoreType.DMA((11,)),
            pltpu.SemaphoreType.DMA((13,)),
        ],
        compiler_params=pltpu.CompilerParams(
            collective_id=0, has_side_effects=True, vmem_limit_bytes=40 << 20
        ),
        name="mixer",
    )(*[pltpu.with_memory_space_constraint(x, pltpu.HBM) for x in operands])
    out = pl.pallas_call(
        store_kernel,
        out_shape=[
            wide,
            wide,
            wide,
            wide,
            f32_wide,
            jax.ShapeDtypeStruct((3, channels), F32),
            jax.ShapeDtypeStruct((channels,), F32),
        ],
        in_specs=[near] * 7,
        out_specs=[far] * 7,
        scratch_shapes=[
            pltpu.VMEM((rows, channels), F32),
            pltpu.VMEM((3, channels), F32),
            pltpu.VMEM((channels,), F32),
            pltpu.SemaphoreType.DMA((10,)),
        ],
        compiler_params=pltpu.CompilerParams(vmem_limit_bytes=16 << 20),
        name="store",
    )(*parts)
    mixed, grad_q, grad_k, grad_v, grad_kernel, grad_short, grad_skip = out
    return mixed, grad_q, grad_k, grad_v, grad_short, grad_skip, grad_kernel


def solution(mesh):
    whole = P("ctx", "ch")
    return jax.shard_map(
        functools.partial(body, (mesh.shape["ctx"], mesh.shape["ch"])),
        mesh=mesh,
        in_specs=(whole, whole, whole, whole, P(None, "ch"), whole, P("ch")),
        out_specs=(whole, whole, whole, whole, P(None, "ch"), P("ch"), whole),
        check_vma=False,
    )
```

```python
import functools
import math

import jax
import jax.numpy as jnp
import numpy as np
from jax import lax
from jax.experimental import pallas as pl
from jax.experimental.pallas import tpu as pltpu
from jax.sharding import PartitionSpec as P

MESH = pl.DeviceIdType.MESH
F32 = jnp.float32
BF16 = jnp.bfloat16
LANES = 128
OWN = 8
HALO, KERN, PROD, BACK, CONV, CORR, LAG, TAIL, SUM1, SUM2, NORM = range(11)


def split_table(table):
    high = table.astype(np.float32).astype(jnp.bfloat16)
    low = (table - high.astype(np.float64)).astype(np.float32).astype(jnp.bfloat16)
    return high, low


def tables(blocks, rows):
    length = blocks * rows
    outer = 2.0 * np.pi * np.outer(np.arange(blocks) + 0.25, np.arange(blocks)) / blocks
    twist = 2.0 * np.pi * np.outer(np.arange(blocks) + 0.25, np.arange(rows)) / length
    inner = 2.0 * np.pi * (np.outer(np.arange(rows), np.arange(rows)) % rows) / rows
    out_f = np.concatenate([np.cos(outer), -np.sin(outer)], axis=0)
    out_i = np.concatenate([np.cos(outer.T), -np.sin(outer.T)], axis=1) / length
    cos, sin = np.cos(inner), np.sin(inner)
    in_f = np.block([[cos, -sin], [sin, cos]])
    in_i = np.block([[cos, sin], [-sin, cos]])
    return (
        np.concatenate(split_table(out_f), axis=1),
        np.concatenate(split_table(out_i), axis=1),
        *split_table(in_f),
        *split_table(in_i),
        np.cos(twist).astype(np.float32),
        np.sin(twist).astype(np.float32),
    )


def by_distance(size):
    return sorted(range(size), key=lambda k: -min(k, size - k))


def mixer_kernel(
    dims,
    limit,
    *refs,
):
    inputs, refs = refs[:15], refs[15:]
    outputs, refs = refs[:7], refs[7:]
    loaded, refs = refs[:15], refs[15:]
    (
    kern_ref,
    k_ref,
    v_ref,
    q_ref,
    go_ref,
    taps_ref,
    outf_ref,
    inf_ref,
    inf_low_ref,
    tcos_ref,
    tsin_ref,
    outi_ref,
    ini_ref,
    ini_low_ref,
    skip_ref,
    ) = loaded
    (
    mixed_ref,
    gq_ref,
    gk_ref,
    gv_ref,
    lag_ref,
    small_ref,
    factor_ref,
    ) = outputs
    (
    src,
    dst,
    ext,
    go_wide,
    corr,
    wide,
    back,
    hsrc,
    hdst,
    tsrc,
    tdst,
    tmp,
    bbuf,
    blow,
    spec,
    weight,
    part,
    part2,
    red1,
    red2,
    nrm,
    nrmd,
    ssem,
    rsem,
    isem,
    ) = refs
    pieces, group_a, group_b, chs = dims
    rows, channels = q_ref.shape
    me = lax.axis_index("ctx")
    ch = lax.axis_index("ch")
    my_a = me // (2 * group_b) * 2 + me % 2
    my_b = me // 2 % group_b

    def ctx_of(a, b):
        return (a // 2 * group_b + b) * 2 + a % 2

    others = [k for k in by_distance(group_a) if k]
    corners = {k: ctx_of(lax.rem(my_a + k, group_a), 0) for k in range(group_a)}

    def each_peer(visit):
        @pl.loop(0, group_b - 1)
        def _(i):
            ahead = i // 2 * (1 - i % 2) - (i + 1) // 2 * (i % 2)
            b = lax.rem(my_b + group_b // 2 + ahead, group_b)
            for k in by_distance(group_a):
                visit(corners[k] + 2 * b)

        for k in others:
            visit(corners[k] + 2 * my_b)

    barrier = pltpu.get_barrier_semaphore()

    def greet(a, b):
        pl.semaphore_signal(barrier, inc=1, device_id=(a, b), device_id_type=MESH)

    each_peer(lambda peer: greet(peer, ch))
    for k in by_distance(chs):
        if k:
            greet(me, lax.rem(ch + k, chs))

    loads = [
        pltpu.make_async_copy(far, near, isem.at[i])
        for i, (far, near) in enumerate(zip(inputs, loaded))
    ]
    for load in loads:
        load.start()

    def spread(slot):
        def send(peer):
            pltpu.make_async_remote_copy(
                src.at[slot, peer],
                dst.at[slot, me],
                ssem.at[KERN + slot],
                rsem.at[KERN + slot],
                device_id=(peer, ch),
                device_id_type=MESH,
            ).start()

        each_peer(send)
        dst[slot, me] = src[slot, me]

    def arrived(slot):
        view = dst.at[slot, pl.ds(0, pieces - 1)]
        pltpu.make_async_copy(view, view, rsem.at[KERN + slot]).wait()

    def to_pieces(slot, cb, block):
        per = LANES // OWN
        src[slot, cb * per : (cb + 1) * per] = block.T.reshape(per, OWN, rows).astype(BF16)

    def from_pieces(slot, cb):
        per = LANES // OWN
        block = dst[slot, cb * per : (cb + 1) * per].astype(F32)
        return block.reshape(LANES, rows).T

    blocks = [slice(cb * LANES, (cb + 1) * LANES) for cb in range(channels // LANES)]

    loads[0].wait()
    for cb, cs in enumerate(blocks):
        to_pieces(0, cb, kern_ref[:, cs])
    for i, (ref, order) in enumerate(((q_ref, 3), (k_ref, 1), (v_ref, 2))):
        loads[order].wait()
        hsrc[2 * i : 2 * i + 2, :] = ref[rows - 16 :, :].astype(F32)[14:16]
    hsrc[6:8, :] = jnp.zeros((2, channels), F32)

    pl.semaphore_wait(barrier, pieces - 1 + chs - 1)

    halo = pltpu.make_async_remote_copy(
        hsrc,
        hdst,
        ssem.at[HALO],
        rsem.at[HALO],
        device_id=(lax.rem(me + 1, pieces), ch),
        device_id_type=MESH,
    )
    halo.start()
    spread(0)
    ext[:, 0:8, :] = jnp.zeros((3, 8, channels), F32)
    for i, ref in enumerate((q_ref, k_ref, v_ref)):
        ext[i, 8 : 8 + rows, :] = ref[...].astype(F32)
    for load in loads[4:]:
        load.wait()

    def short(i, first, count, cs):
        total = taps_ref[0:1, cs] * ext[i, 8 + first : 8 + first + count, cs]
        for j in range(1, 3):
            start = 8 - j + first
            total = total + taps_ref[j : j + 1, cs] * ext[i, start : start + count, cs]
        return total

    def local_part(first, count, cs):
        here = slice(first, first + count)
        q_short, k_short, v_short = (short(i, first, count, cs) for i in range(3))
        wide[0, here, cs] = q_short
        wide[1, here, cs] = k_short
        wide[2, here, cs] = v_short
        wide[3, here, cs] = (k_short * v_short).astype(BF16).astype(F32)
        wide[4, here, cs] = go_wide[here, cs] * q_short

    go_wide[...] = go_ref[...].astype(F32)
    for cs in blocks:
        local_part(0, rows, cs)
    halo.wait_recv()
    for i in range(3):
        halo_rows = hdst[2 * i : 2 * i + 2, :]
        ext[i, 6:8, :] = jnp.where(me > 0, halo_rows, jnp.zeros_like(halo_rows))
    for cs in blocks:
        local_part(0, 8, cs)
    for cb, cs in enumerate(blocks):
        to_pieces(1, cb, wide[3, :, cs])
    spread(1)
    for cb, cs in enumerate(blocks):
        to_pieces(2, cb, wide[4, :, cs])
    spread(2)

    for cs in blocks:
        back_mix = wide[4, :, cs]
        part[3:4, cs] = jnp.sum(back_mix * wide[3, :, cs], axis=0, keepdims=True)
        for j in range(3):
            here = slice(8 - j, 8 - j + rows)
            pair = wide[2, :, cs] * ext[1, here, cs] + wide[1, :, cs] * ext[2, here, cs]
            weight[j, :, cs] = pair
            part[j : j + 1, cs] = skip_ref[:, cs] * jnp.sum(
                back_mix * pair, axis=0, keepdims=True
            )

    def put(here, columns, value, precise):
        high = value.astype(BF16)
        bbuf[here, columns] = high
        if precise:
            blow[here, columns] = (value - high.astype(F32)).astype(BF16)

    def inner(high, low, precise):
        total = jnp.dot(bbuf[...], high[...], preferred_element_type=F32)
        if precise:
            total = total + jnp.dot(bbuf[...], low[...], preferred_element_type=F32)
            total = total + jnp.dot(blow[...], high[...], preferred_element_type=F32)
        return total

    left_half, right_half = slice(0, rows), slice(rows, 2 * rows)

    def transform(slot, precise):
        tmp[...] = dst[slot].astype(F32).reshape(pieces * OWN, rows)
        cols = [tmp[pl.ds(c, pieces, stride=OWN), :] for c in range(OWN)]
        signal = jnp.concatenate(cols, axis=1).astype(BF16)
        outer = jnp.dot(
            outf_ref[...],
            jnp.concatenate([signal, signal], axis=0),
            preferred_element_type=F32,
        )
        cos, sin = tcos_ref[...], tsin_ref[...]
        for c in range(OWN):
            re = outer[:pieces, c * rows : (c + 1) * rows]
            im = outer[pieces:, c * rows : (c + 1) * rows]
            here = slice(c * pieces, (c + 1) * pieces)
            put(here, left_half, re * cos + im * sin, precise)
            put(here, right_half, im * cos - re * sin, precise)
        spec[slot] = inner(inf_ref, inf_low_ref, precise)

    def inverse(slot, left, right, conj, precise):
        a_re, a_im = spec[left, :, :rows], spec[left, :, rows:]
        b_re, b_im = spec[right, :, :rows], spec[right, :, rows:]
        if conj:
            a_im = -a_im
        put(slice(None), left_half, a_re * b_re - a_im * b_im, precise)
        put(slice(None), right_half, a_re * b_im + a_im * b_re, precise)
        turned = inner(ini_ref, ini_low_ref, precise)
        cos, sin = tcos_ref[...], tsin_ref[...]
        cols = []
        for c in range(OWN):
            re = turned[c * pieces : (c + 1) * pieces, :rows]
            im = turned[c * pieces : (c + 1) * pieces, rows:]
            cols.append(jnp.concatenate([re * cos - im * sin, im * cos + re * sin], axis=0))
        turned = jnp.concatenate(cols, axis=1)
        high = turned.astype(BF16)
        out = jnp.dot(
            outi_ref[...],
            jnp.concatenate([high, high], axis=0),
            preferred_element_type=F32,
        )
        if precise:
            low = (turned - high.astype(F32)).astype(BF16)
            out = out + jnp.dot(outi_ref[:, : 2 * pieces], low, preferred_element_type=F32)
        for c in range(OWN):
            tmp[pl.ds(c, pieces, stride=OWN), :] = out[:, c * rows : (c + 1) * rows]
        src[slot] = tmp[...].reshape(pieces, OWN, rows).astype(BF16)
        return out

    arrived(0)
    transform(0, True)
    arrived(1)
    transform(1, False)
    inverse(3, 0, 1, False, False)
    spread(3)
    arrived(2)
    transform(2, False)
    inverse(4, 0, 2, True, False)
    spread(4)
    lag = inverse(5, 1, 2, True, True)
    spread(5)
    square = jnp.sum(lag * lag, axis=0, keepdims=True)
    part[:, channels:] = jnp.zeros((4, LANES), F32)
    part[0:1, channels:] = sum(square[:, c * rows : (c + 1) * rows] for c in range(OWN))

    arrived(3)
    for cb, cs in enumerate(blocks):
        filtered = from_pieces(3, cb) + skip_ref[:, cs] * wide[3, :, cs]
        mixed_ref[:, cs] = (wide[0, :, cs] * filtered).astype(BF16)
        back_q = go_wide[:, cs] * filtered
        back[0, :rows, cs] = back_q
        for j in range(3):
            part[j : j + 1, cs] += jnp.sum(
                back_q * ext[0, 8 - j : 8 - j + rows, cs], axis=0, keepdims=True
            )
    arrived(4)
    for cb, cs in enumerate(blocks):
        block = from_pieces(4, cb)
        corr[:, cs] = block
        for j in range(3):
            part[j : j + 1, cs] += jnp.sum(block * weight[j, :, cs], axis=0, keepdims=True)

    def exchange(source, slots, mine, size, sem, device_of):
        for k in by_distance(size):
            if k:
                pltpu.make_async_remote_copy(
                    source,
                    slots.at[mine],
                    ssem.at[sem],
                    rsem.at[sem],
                    device_id=device_of(lax.rem(mine + k, size)),
                    device_id_type=MESH,
                ).start()
        slots[mine] = source[...]

    def wait_many(slots, size, sem):
        view = slots.at[pl.ds(0, size - 1)]
        pltpu.make_async_copy(view, view, sem).wait()

    def total_of(slots, size, sem):
        wait_many(slots, size, rsem.at[sem])
        total = slots[0]
        for i in range(1, size):
            total = total + slots[i]
        return total

    exchange(part, red1, my_a, group_a, SUM1, lambda peer: (ctx_of(peer, my_b), ch))
    for cs in blocks:
        back_prod = corr[:, cs] + skip_ref[:, cs] * wide[4, :, cs]
        back[1, :rows, cs] = back_prod * wide[2, :, cs]
        back[2, :rows, cs] = back_prod * wide[1, :, cs]

    for i in range(3):
        tsrc[2 * i : 2 * i + 2, :] = back[i, 0:2, :]
    tsrc[6:8, :] = jnp.zeros((2, channels), F32)
    tail = pltpu.make_async_remote_copy(
        tsrc,
        tdst,
        ssem.at[TAIL],
        rsem.at[TAIL],
        device_id=(lax.rem(me + pieces - 1, pieces), ch),
        device_id_type=MESH,
    )
    tail.start()

    sums = total_of(red1, group_a, SUM1)
    part2[...] = sums
    exchange(part2, red2, my_b, group_b, SUM2, lambda peer: (ctx_of(my_a, peer), ch))

    tail.wait_recv()
    for i, ref in enumerate((gq_ref, gk_ref, gv_ref)):
        tail_rows = tdst[2 * i : 2 * i + 2, :]
        back[i, rows : rows + 2, :] = jnp.where(
            me < pieces - 1, tail_rows, jnp.zeros_like(tail_rows)
        )
        for cs in blocks:
            total = taps_ref[0:1, cs] * back[i, 0:rows, cs]
            for j in range(1, 3):
                total = total + taps_ref[j : j + 1, cs] * back[i, j : j + rows, cs]
            ref[:, cs] = total.astype(BF16)

    sums = total_of(red2, group_b, SUM2)
    squares = sums[:, :channels] * sums[:, :channels]
    square = jnp.sum(squares, keepdims=True) + jnp.sum(sums[:, channels:], keepdims=True)
    nrm[...] = jnp.broadcast_to(square, nrm.shape)
    exchange(nrm, nrmd, ch, chs, NORM, lambda peer: (me, peer))
    small_ref[...] = sums[:, :channels]

    arrived(5)
    for cb, cs in enumerate(blocks):
        lag_ref[:, cs] = from_pieces(5, cb)

    norm_sq = total_of(nrmd, chs, NORM)
    factor_ref[...] = limit / jnp.maximum(jnp.sqrt(norm_sq), limit)

    wait_many(red1, group_a, ssem.at[SUM1])
    wait_many(red2, group_b, ssem.at[SUM2])
    wait_many(nrmd, chs, ssem.at[NORM])
    halo.wait_send()
    tail.wait_send()
    for slot in range(6):
        view = src.at[slot, pl.ds(0, pieces - 1)]
        pltpu.make_async_copy(view, view, ssem.at[KERN + slot]).wait()


def store_kernel(*refs):
    near, far, (kern, short, skip, sem) = refs[:7], refs[7:14], refs[14:]
    lag_ref, small_ref, factor_ref = near[4:]
    copies = [pltpu.make_async_copy(a, b, sem.at[i]) for i, (a, b) in enumerate(zip(near[:4], far))]
    for copy in copies:
        copy.start()
    factor = factor_ref[0:1, 0:1]
    step = kern.shape[0] // 4
    for i in range(4):
        here = pl.ds(i * step, step)
        kern[here, :] = factor * lag_ref[here, :]
        copies.append(pltpu.make_async_copy(kern.at[here], far[4].at[here], sem.at[4 + i]))
        copies[-1].start()
    short[...] = factor * small_ref[0:3, :]
    skip[...] = (factor * small_ref[3:4, :]).reshape(skip.shape)
    for i, (a, b) in enumerate(((short, far[5]), (skip, far[6]))):
        copies.append(pltpu.make_async_copy(a, b, sem.at[8 + i]))
        copies[-1].start()
    for copy in copies:
        copy.wait()


def body(sizes, q_in, k_in, v_in, grad_out, short_filter, kernel, skip):
    pieces, chs = sizes
    rows, channels = q_in.shape
    group_a = group_b = math.isqrt(pieces)
    limit = math.sqrt(float(pieces * rows * channels * chs))
    consts = [jnp.asarray(table) for table in tables(pieces, rows)]
    wide = jax.ShapeDtypeStruct((rows, channels), BF16)
    far = pl.BlockSpec(memory_space=pltpu.HBM)
    near = pl.BlockSpec(memory_space=pltpu.VMEM)
    operands = [kernel, k_in, v_in, q_in, grad_out, short_filter]
    operands += [consts[i] for i in (0, 2, 3, 6, 7, 1, 4, 5)]
    operands.append(skip[None, :])
    f32_wide = jax.ShapeDtypeStruct((rows, channels), F32)
    results = [
        wide,
        wide,
        wide,
        wide,
        f32_wide,
        jax.ShapeDtypeStruct((4, channels), F32),
        jax.ShapeDtypeStruct((1, LANES), F32),
    ]
    parts = pl.pallas_call(
        functools.partial(mixer_kernel, (pieces, group_a, group_b, chs), limit),
        out_shape=results,
        in_specs=[far] * 15,
        out_specs=[near] * 7,
        scratch_shapes=[
            *(pltpu.VMEM(x.shape, x.dtype) for x in operands),
            pltpu.VMEM((6, pieces, OWN, rows), BF16),
            pltpu.VMEM((6, pieces, OWN, rows), BF16),
            pltpu.VMEM((3, rows + 8, channels), F32),
            pltpu.VMEM((rows, channels), F32),
            pltpu.VMEM((rows, channels), F32),
            pltpu.VMEM((5, rows, channels), F32),
            pltpu.VMEM((3, rows + 8, channels), F32),
            *(pltpu.VMEM((8, channels), F32) for _ in range(4)),
            pltpu.VMEM((pieces * OWN, rows), F32),
            pltpu.VMEM((pieces * OWN, 2 * rows), BF16),
            pltpu.VMEM((pieces * OWN, 2 * rows), BF16),
            pltpu.VMEM((3, pieces * OWN, 2 * rows), F32),
            pltpu.VMEM((3, rows, channels), F32),
            pltpu.VMEM((4, channels + LANES), F32),
            pltpu.VMEM((4, channels + LANES), F32),
            pltpu.VMEM((group_a, 4, channels + LANES), F32),
            pltpu.VMEM((group_b, 4, channels + LANES), F32),
            pltpu.VMEM((1, LANES), F32),
            pltpu.VMEM((chs, 1, LANES), F32),
            pltpu.SemaphoreType.DMA((11,)),
            pltpu.SemaphoreType.DMA((11,)),
            pltpu.SemaphoreType.DMA((15,)),
        ],
        compiler_params=pltpu.CompilerParams(
            collective_id=0, has_side_effects=True, vmem_limit_bytes=40 << 20
        ),
        name="mixer",
    )(*[pltpu.with_memory_space_constraint(x, pltpu.HBM) for x in operands])
    out = pl.pallas_call(
        store_kernel,
        out_shape=[
            wide,
            wide,
            wide,
            wide,
            f32_wide,
            jax.ShapeDtypeStruct((3, channels), F32),
            jax.ShapeDtypeStruct((channels,), F32),
        ],
        in_specs=[near] * 7,
        out_specs=[far] * 7,
        scratch_shapes=[
            pltpu.VMEM((rows, channels), F32),
            pltpu.VMEM((3, channels), F32),
            pltpu.VMEM((channels,), F32),
            pltpu.SemaphoreType.DMA((10,)),
        ],
        compiler_params=pltpu.CompilerParams(vmem_limit_bytes=16 << 20),
        name="store",
    )(*parts)
    mixed, grad_q, grad_k, grad_v, grad_kernel, grad_short, grad_skip = out
    return mixed, grad_q, grad_k, grad_v, grad_short, grad_skip, grad_kernel


def solution(mesh):
    whole = P("ctx", "ch")
    return jax.shard_map(
        functools.partial(body, (mesh.shape["ctx"], mesh.shape["ch"])),
        mesh=mesh,
        in_specs=(whole, whole, whole, whole, P(None, "ch"), whole, P("ch")),
        out_specs=(whole, whole, whole, whole, P(None, "ch"), P("ch"), whole),
        check_vma=False,
    )
```

```python
import functools
import math

import jax
import jax.numpy as jnp
import numpy as np
from jax import lax
from jax.experimental import pallas as pl
from jax.experimental.pallas import tpu as pltpu
from jax.sharding import PartitionSpec as P

MESH = pl.DeviceIdType.MESH
F32 = jnp.float32
BF16 = jnp.bfloat16
LANES = 128
OWN = 8
HALO, KERN, PROD, BACK, CONV, CORR, LAG, TAIL, SUM1, SUM2, NORM = range(11)


def split_table(table):
    high = table.astype(np.float32).astype(jnp.bfloat16)
    low = (table - high.astype(np.float64)).astype(np.float32).astype(jnp.bfloat16)
    return high, low


def tables(blocks, rows):
    length = blocks * rows
    outer = 2.0 * np.pi * np.outer(np.arange(blocks) + 0.25, np.arange(blocks)) / blocks
    twist = 2.0 * np.pi * np.outer(np.arange(blocks) + 0.25, np.arange(rows)) / length
    inner = 2.0 * np.pi * (np.outer(np.arange(rows), np.arange(rows)) % rows) / rows
    out_f = np.concatenate([np.cos(outer), -np.sin(outer)], axis=0)
    out_i = np.concatenate([np.cos(outer.T), -np.sin(outer.T)], axis=1) / length
    cos, sin = np.cos(inner), np.sin(inner)
    in_f = np.block([[cos, -sin], [sin, cos]])
    in_i = np.block([[cos, sin], [-sin, cos]])
    return (
        np.concatenate(split_table(out_f), axis=1),
        np.concatenate(split_table(out_i), axis=1),
        *split_table(in_f),
        *split_table(in_i),
        np.cos(twist).astype(np.float32),
        np.sin(twist).astype(np.float32),
    )


def by_distance(size):
    return sorted(range(size), key=lambda k: -min(k, size - k))


def mixer_kernel(
    dims,
    limit,
    *refs,
):
    inputs, refs = refs[:15], refs[15:]
    outputs, refs = refs[:7], refs[7:]
    loaded, refs = refs[:15], refs[15:]
    (
    kern_ref,
    k_ref,
    v_ref,
    q_ref,
    go_ref,
    taps_ref,
    outf_ref,
    inf_ref,
    inf_low_ref,
    tcos_ref,
    tsin_ref,
    outi_ref,
    ini_ref,
    ini_low_ref,
    skip_ref,
    ) = loaded
    (
    mixed_ref,
    gq_ref,
    gk_ref,
    gv_ref,
    lag_ref,
    small_ref,
    factor_ref,
    ) = outputs
    (
    src,
    dst,
    ext,
    go_wide,
    corr,
    wide,
    back,
    hsrc,
    hdst,
    tsrc,
    tdst,
    tmp,
    bbuf,
    blow,
    spec,
    weight,
    part,
    part2,
    red1,
    red2,
    nrm,
    nrmd,
    ssem,
    rsem,
    isem,
    ) = refs
    pieces, group_a, group_b, chs = dims
    rows, channels = q_ref.shape
    me = lax.axis_index("ctx")
    ch = lax.axis_index("ch")
    my_a = me // (2 * group_b) * 2 + me % 2
    my_b = me // 2 % group_b

    def ctx_of(a, b):
        return (a // 2 * group_b + b) * 2 + a % 2

    others = [k for k in by_distance(group_a) if k]
    corners = {k: ctx_of(lax.rem(my_a + k, group_a), 0) for k in range(group_a)}

    def each_peer(visit):
        @pl.loop(0, group_b - 1)
        def _(i):
            ahead = i // 2 * (1 - i % 2) - (i + 1) // 2 * (i % 2)
            b = lax.rem(my_b + group_b // 2 + ahead, group_b)
            for k in by_distance(group_a):
                visit(corners[k] + 2 * b)

        for k in others:
            visit(corners[k] + 2 * my_b)

    barrier = pltpu.get_barrier_semaphore()

    def greet(a, b):
        pl.semaphore_signal(barrier, inc=1, device_id=(a, b), device_id_type=MESH)

    each_peer(lambda peer: greet(peer, ch))
    for k in by_distance(chs):
        if k:
            greet(me, lax.rem(ch + k, chs))

    loads = [
        pltpu.make_async_copy(far, near, isem.at[i])
        for i, (far, near) in enumerate(zip(inputs, loaded))
    ]
    for load in loads:
        load.start()

    def spread(slot):
        def send(peer):
            pltpu.make_async_remote_copy(
                src.at[slot, peer],
                dst.at[slot, me],
                ssem.at[KERN + slot],
                rsem.at[KERN + slot],
                device_id=(peer, ch),
                device_id_type=MESH,
            ).start()

        each_peer(send)
        dst[slot, me] = src[slot, me]

    def arrived(slot):
        view = dst.at[slot, pl.ds(0, pieces - 1)]
        pltpu.make_async_copy(view, view, rsem.at[KERN + slot]).wait()

    def to_pieces(slot, cb, block):
        per = LANES // OWN
        src[slot, cb * per : (cb + 1) * per] = (
            block.astype(BF16).T.astype(F32).reshape(per, OWN, rows).astype(BF16)
        )

    def from_pieces(slot, cb):
        per = LANES // OWN
        block = dst[slot, cb * per : (cb + 1) * per].astype(F32)
        return block.reshape(LANES, rows).T

    blocks = [slice(cb * LANES, (cb + 1) * LANES) for cb in range(channels // LANES)]

    loads[0].wait()
    for cb, cs in enumerate(blocks):
        to_pieces(0, cb, kern_ref[:, cs])
    for i, (ref, order) in enumerate(((q_ref, 3), (k_ref, 1), (v_ref, 2))):
        loads[order].wait()
        hsrc[2 * i : 2 * i + 2, :] = ref[rows - 16 :, :].astype(F32)[14:16]
    hsrc[6:8, :] = jnp.zeros((2, channels), F32)

    pl.semaphore_wait(barrier, pieces - 1 + chs - 1)

    halo = pltpu.make_async_remote_copy(
        hsrc,
        hdst,
        ssem.at[HALO],
        rsem.at[HALO],
        device_id=(lax.rem(me + 1, pieces), ch),
        device_id_type=MESH,
    )
    halo.start()
    spread(0)
    ext[:, 0:8, :] = jnp.zeros((3, 8, channels), F32)
    for i, ref in enumerate((q_ref, k_ref, v_ref)):
        ext[i, 8 : 8 + rows, :] = ref[...].astype(F32)
    for load in loads[4:]:
        load.wait()

    def short(i, first, count, cs):
        total = taps_ref[0:1, cs] * ext[i, 8 + first : 8 + first + count, cs]
        for j in range(1, 3):
            start = 8 - j + first
            total = total + taps_ref[j : j + 1, cs] * ext[i, start : start + count, cs]
        return total

    def local_part(first, count, cs):
        here = slice(first, first + count)
        q_short, k_short, v_short = (short(i, first, count, cs) for i in range(3))
        wide[0, here, cs] = q_short
        wide[1, here, cs] = k_short
        wide[2, here, cs] = v_short
        wide[3, here, cs] = (k_short * v_short).astype(BF16).astype(F32)
        wide[4, here, cs] = go_wide[here, cs] * q_short

    go_wide[...] = go_ref[...].astype(F32)
    for cs in blocks:
        local_part(0, rows, cs)
    halo.wait_recv()
    for i in range(3):
        halo_rows = hdst[2 * i : 2 * i + 2, :]
        ext[i, 6:8, :] = jnp.where(me > 0, halo_rows, jnp.zeros_like(halo_rows))
    for cs in blocks:
        local_part(0, 8, cs)
    for cb, cs in enumerate(blocks):
        to_pieces(1, cb, wide[3, :, cs])
    spread(1)
    for cb, cs in enumerate(blocks):
        to_pieces(2, cb, wide[4, :, cs])
    spread(2)

    for cs in blocks:
        back_mix = wide[4, :, cs]
        part[3:4, cs] = jnp.sum(back_mix * wide[3, :, cs], axis=0, keepdims=True)
        for j in range(3):
            here = slice(8 - j, 8 - j + rows)
            pair = wide[2, :, cs] * ext[1, here, cs] + wide[1, :, cs] * ext[2, here, cs]
            weight[j, :, cs] = pair
            part[j : j + 1, cs] = skip_ref[:, cs] * jnp.sum(
                back_mix * pair, axis=0, keepdims=True
            )

    def put(here, columns, value, precise):
        high = value.astype(BF16)
        bbuf[here, columns] = high
        if precise:
            blow[here, columns] = (value - high.astype(F32)).astype(BF16)

    def inner(high, low, precise):
        total = jnp.dot(bbuf[...], high[...], preferred_element_type=F32)
        if precise:
            total = total + jnp.dot(bbuf[...], low[...], preferred_element_type=F32)
            total = total + jnp.dot(blow[...], high[...], preferred_element_type=F32)
        return total

    left_half, right_half = slice(0, rows), slice(rows, 2 * rows)

    def transform(slot, precise):
        tmp[...] = dst[slot].astype(F32).reshape(pieces * OWN, rows)
        cols = [tmp[pl.ds(c, pieces, stride=OWN), :] for c in range(OWN)]
        signal = jnp.concatenate(cols, axis=1).astype(BF16)
        outer = jnp.dot(
            outf_ref[...],
            jnp.concatenate([signal, signal], axis=0),
            preferred_element_type=F32,
        )
        cos, sin = tcos_ref[...], tsin_ref[...]
        for c in range(OWN):
            re = outer[:pieces, c * rows : (c + 1) * rows]
            im = outer[pieces:, c * rows : (c + 1) * rows]
            here = slice(c * pieces, (c + 1) * pieces)
            put(here, left_half, re * cos + im * sin, precise)
            put(here, right_half, im * cos - re * sin, precise)
        spec[slot] = inner(inf_ref, inf_low_ref, precise)

    def inverse(slot, left, right, conj, precise):
        a_re, a_im = spec[left, :, :rows], spec[left, :, rows:]
        b_re, b_im = spec[right, :, :rows], spec[right, :, rows:]
        if conj:
            a_im = -a_im
        put(slice(None), left_half, a_re * b_re - a_im * b_im, precise)
        put(slice(None), right_half, a_re * b_im + a_im * b_re, precise)
        turned = inner(ini_ref, ini_low_ref, precise)
        cos, sin = tcos_ref[...], tsin_ref[...]
        cols = []
        for c in range(OWN):
            re = turned[c * pieces : (c + 1) * pieces, :rows]
            im = turned[c * pieces : (c + 1) * pieces, rows:]
            cols.append(jnp.concatenate([re * cos - im * sin, im * cos + re * sin], axis=0))
        turned = jnp.concatenate(cols, axis=1)
        high = turned.astype(BF16)
        out = jnp.dot(
            outi_ref[...],
            jnp.concatenate([high, high], axis=0),
            preferred_element_type=F32,
        )
        if precise:
            low = (turned - high.astype(F32)).astype(BF16)
            out = out + jnp.dot(outi_ref[:, : 2 * pieces], low, preferred_element_type=F32)
        for c in range(OWN):
            tmp[pl.ds(c, pieces, stride=OWN), :] = out[:, c * rows : (c + 1) * rows]
        src[slot] = tmp[...].reshape(pieces, OWN, rows).astype(BF16)
        return out

    arrived(0)
    transform(0, True)
    arrived(1)
    transform(1, False)
    inverse(3, 0, 1, False, False)
    spread(3)
    arrived(2)
    transform(2, False)
    inverse(4, 0, 2, True, False)
    spread(4)
    lag = inverse(5, 1, 2, True, True)
    spread(5)
    square = jnp.sum(lag * lag, axis=0, keepdims=True)
    part[:, channels:] = jnp.zeros((4, LANES), F32)
    part[0:1, channels:] = sum(square[:, c * rows : (c + 1) * rows] for c in range(OWN))

    arrived(3)
    for cb, cs in enumerate(blocks):
        filtered = from_pieces(3, cb) + skip_ref[:, cs] * wide[3, :, cs]
        mixed_ref[:, cs] = (wide[0, :, cs] * filtered).astype(BF16)
        back_q = go_wide[:, cs] * filtered
        back[0, :rows, cs] = back_q
        for j in range(3):
            part[j : j + 1, cs] += jnp.sum(
                back_q * ext[0, 8 - j : 8 - j + rows, cs], axis=0, keepdims=True
            )
    arrived(4)
    for cb, cs in enumerate(blocks):
        block = from_pieces(4, cb)
        corr[:, cs] = block
        for j in range(3):
            part[j : j + 1, cs] += jnp.sum(block * weight[j, :, cs], axis=0, keepdims=True)

    def exchange(source, slots, mine, size, sem, device_of):
        for k in by_distance(size):
            if k:
                pltpu.make_async_remote_copy(
                    source,
                    slots.at[mine],
                    ssem.at[sem],
                    rsem.at[sem],
                    device_id=device_of(lax.rem(mine + k, size)),
                    device_id_type=MESH,
                ).start()
        slots[mine] = source[...]

    def wait_many(slots, size, sem):
        view = slots.at[pl.ds(0, size - 1)]
        pltpu.make_async_copy(view, view, sem).wait()

    def total_of(slots, size, sem):
        wait_many(slots, size, rsem.at[sem])
        total = slots[0]
        for i in range(1, size):
            total = total + slots[i]
        return total

    exchange(part, red1, my_a, group_a, SUM1, lambda peer: (ctx_of(peer, my_b), ch))
    for cs in blocks:
        back_prod = corr[:, cs] + skip_ref[:, cs] * wide[4, :, cs]
        back[1, :rows, cs] = back_prod * wide[2, :, cs]
        back[2, :rows, cs] = back_prod * wide[1, :, cs]

    for i in range(3):
        tsrc[2 * i : 2 * i + 2, :] = back[i, 0:2, :]
    tsrc[6:8, :] = jnp.zeros((2, channels), F32)
    tail = pltpu.make_async_remote_copy(
        tsrc,
        tdst,
        ssem.at[TAIL],
        rsem.at[TAIL],
        device_id=(lax.rem(me + pieces - 1, pieces), ch),
        device_id_type=MESH,
    )
    tail.start()

    sums = total_of(red1, group_a, SUM1)
    part2[...] = sums
    exchange(part2, red2, my_b, group_b, SUM2, lambda peer: (ctx_of(my_a, peer), ch))

    tail.wait_recv()
    for i, ref in enumerate((gq_ref, gk_ref, gv_ref)):
        tail_rows = tdst[2 * i : 2 * i + 2, :]
        back[i, rows : rows + 2, :] = jnp.where(
            me < pieces - 1, tail_rows, jnp.zeros_like(tail_rows)
        )
        for cs in blocks:
            total = taps_ref[0:1, cs] * back[i, 0:rows, cs]
            for j in range(1, 3):
                total = total + taps_ref[j : j + 1, cs] * back[i, j : j + rows, cs]
            ref[:, cs] = total.astype(BF16)

    sums = total_of(red2, group_b, SUM2)
    squares = sums[:, :channels] * sums[:, :channels]
    square = sum(squares[:, b] for b in blocks) + sums[:, channels:]
    square = jnp.sum(square, axis=0, keepdims=True)
    nrm[...] = square
    exchange(nrm, nrmd, ch, chs, NORM, lambda peer: (me, peer))
    small_ref[...] = sums[:, :channels]

    arrived(5)
    for cb, cs in enumerate(blocks):
        lag_ref[:, cs] = from_pieces(5, cb)

    norm_sq = jnp.sum(total_of(nrmd, chs, NORM), keepdims=True)
    factor = limit / jnp.maximum(jnp.sqrt(norm_sq), limit)
    factor_ref[...] = jnp.broadcast_to(factor, factor_ref.shape)

    wait_many(red1, group_a, ssem.at[SUM1])
    wait_many(red2, group_b, ssem.at[SUM2])
    wait_many(nrmd, chs, ssem.at[NORM])
    halo.wait_send()
    tail.wait_send()
    for slot in range(6):
        view = src.at[slot, pl.ds(0, pieces - 1)]
        pltpu.make_async_copy(view, view, ssem.at[KERN + slot]).wait()


def store_kernel(*refs):
    near, far, (kern, short, skip, sem) = refs[:7], refs[7:14], refs[14:]
    lag_ref, small_ref, factor_ref = near[4:]
    copies = [pltpu.make_async_copy(a, b, sem.at[i]) for i, (a, b) in enumerate(zip(near[:4], far))]
    factor = factor_ref[0:1, 0:1]
    step = kern.shape[0] // 4
    for i in range(4):
        here = pl.ds(i * step, step)
        kern[here, :] = factor * lag_ref[here, :]
        copies.append(pltpu.make_async_copy(kern.at[here], far[4].at[here], sem.at[4 + i]))
        copies[-1].start()
    for copy in copies[:4]:
        copy.start()
    short[...] = factor * small_ref[0:3, :]
    skip[...] = (factor * small_ref[3:4, :]).reshape(skip.shape)
    for i, (a, b) in enumerate(((short, far[5]), (skip, far[6]))):
        copies.append(pltpu.make_async_copy(a, b, sem.at[8 + i]))
        copies[-1].start()
    for copy in copies:
        copy.wait()


def body(sizes, q_in, k_in, v_in, grad_out, short_filter, kernel, skip):
    pieces, chs = sizes
    rows, channels = q_in.shape
    group_a = group_b = math.isqrt(pieces)
    limit = math.sqrt(float(pieces * rows * channels * chs))
    consts = [jnp.asarray(table) for table in tables(pieces, rows)]
    wide = jax.ShapeDtypeStruct((rows, channels), BF16)
    far = pl.BlockSpec(memory_space=pltpu.HBM)
    near = pl.BlockSpec(memory_space=pltpu.VMEM)
    operands = [kernel, k_in, v_in, q_in, grad_out, short_filter]
    operands += [consts[i] for i in (0, 2, 3, 6, 7, 1, 4, 5)]
    operands.append(skip[None, :])
    f32_wide = jax.ShapeDtypeStruct((rows, channels), F32)
    results = [
        wide,
        wide,
        wide,
        wide,
        f32_wide,
        jax.ShapeDtypeStruct((4, channels), F32),
        jax.ShapeDtypeStruct((1, LANES), F32),
    ]
    parts = pl.pallas_call(
        functools.partial(mixer_kernel, (pieces, group_a, group_b, chs), limit),
        out_shape=results,
        in_specs=[far] * 15,
        out_specs=[near] * 7,
        scratch_shapes=[
            *(pltpu.VMEM(x.shape, x.dtype) for x in operands),
            pltpu.VMEM((6, pieces, OWN, rows), BF16),
            pltpu.VMEM((6, pieces, OWN, rows), BF16),
            pltpu.VMEM((3, rows + 8, channels), F32),
            pltpu.VMEM((rows, channels), F32),
            pltpu.VMEM((rows, channels), F32),
            pltpu.VMEM((5, rows, channels), F32),
            pltpu.VMEM((3, rows + 8, channels), F32),
            *(pltpu.VMEM((8, channels), F32) for _ in range(4)),
            pltpu.VMEM((pieces * OWN, rows), F32),
            pltpu.VMEM((pieces * OWN, 2 * rows), BF16),
            pltpu.VMEM((pieces * OWN, 2 * rows), BF16),
            pltpu.VMEM((3, pieces * OWN, 2 * rows), F32),
            pltpu.VMEM((3, rows, channels), F32),
            pltpu.VMEM((4, channels + LANES), F32),
            pltpu.VMEM((4, channels + LANES), F32),
            pltpu.VMEM((group_a, 4, channels + LANES), F32),
            pltpu.VMEM((group_b, 4, channels + LANES), F32),
            pltpu.VMEM((1, LANES), F32),
            pltpu.VMEM((chs, 1, LANES), F32),
            pltpu.SemaphoreType.DMA((11,)),
            pltpu.SemaphoreType.DMA((11,)),
            pltpu.SemaphoreType.DMA((15,)),
        ],
        compiler_params=pltpu.CompilerParams(
            collective_id=0, has_side_effects=True, vmem_limit_bytes=40 << 20
        ),
        name="mixer",
    )(*[pltpu.with_memory_space_constraint(x, pltpu.HBM) for x in operands])
    out = pl.pallas_call(
        store_kernel,
        out_shape=[
            wide,
            wide,
            wide,
            wide,
            f32_wide,
            jax.ShapeDtypeStruct((3, channels), F32),
            jax.ShapeDtypeStruct((channels,), F32),
        ],
        in_specs=[near] * 7,
        out_specs=[far] * 7,
        scratch_shapes=[
            pltpu.VMEM((rows, channels), F32),
            pltpu.VMEM((3, channels), F32),
            pltpu.VMEM((channels,), F32),
            pltpu.SemaphoreType.DMA((10,)),
        ],
        compiler_params=pltpu.CompilerParams(vmem_limit_bytes=16 << 20),
        name="store",
    )(*parts)
    mixed, grad_q, grad_k, grad_v, grad_kernel, grad_short, grad_skip = out
    return mixed, grad_q, grad_k, grad_v, grad_short, grad_skip, grad_kernel


def solution(mesh):
    whole = P("ctx", "ch")
    return jax.shard_map(
        functools.partial(body, (mesh.shape["ctx"], mesh.shape["ch"])),
        mesh=mesh,
        in_specs=(whole, whole, whole, whole, P(None, "ch"), whole, P("ch")),
        out_specs=(whole, whole, whole, whole, P(None, "ch"), P("ch"), whole),
        check_vma=False,
    )
```
